256 devices in a mesh: gz: 64 (over y, z, core), gy: 4 (over x).
Axes of the slice: x: 4, y: 4, z: 8, core: 2. Of those that a mesh axis runs over, the one named last changes fastest.
Arguments:
- state: bfloat16 [32, 256, 64, 256], P(None, 'gz', 'gy'), may hold values from -6 to 6
- residual: bfloat16 [4096, 4, 768], P('gz'), may hold values from -6 to 6
- projector: bfloat16 [4, 768, 512], replicated, may hold values from -0.21875 to 0.21875
- pair_counts: int32 [4, 64, 7], P('gy'), may hold values from 0 to 32, as said below
- pair_block: int32 [4, 64, 224], P('gy'), may hold values from 0 to 63
- pair_tile: int32 [4, 64, 224], P('gy'), may hold values from 0 to 7
- pair_view: int32 [4, 64, 224], P('gy'), may hold values from 0 to 3
- enc_weight: bfloat16 [2, 2, 2, 64, 33], replicated, may hold values from -0.375 to 0.375
- dec_weight: bfloat16 [4, 4, 4, 32, 64], replicated, may hold values from -0.25 to 0.25
Outputs:
- new_state: bfloat16 [32, 256, 64, 256], P(None, 'gz', 'gy')
The draws below stay inside these ranges and needn't reach their ends.
Inputs may be any that keep to these rules, and one draw needn't show every extreme that they name: pair_counts[j, i, o] is 0 where slab i - 3 + o lies outside 0 .. 63, exactly 32 for o = 3, and 1 to 32 otherwise. The slots of pair_block, pair_tile and pair_view past the last group of a source slab are unused.
All inputs are finite; a program needn't handle non-finite values.
Results may differ from the reference program's by a relative error of at most 0.0054.
Values may be sent and summed in bfloat16 or wider, within the bound.
No kernel may reach another device: no remote copies, remote signals or barrier semaphores. Data moves between devices by JAX's collectives and lax.ppermute only.
A program may use at most 128 MiB of HBM per device.

```python
import jax
import jax.numpy as jnp
from jax import lax

C1 = 32
C2 = 64
ZD = 4
XD = 256
DC = 768
TY = 2
VIEWS = 4
NBD = 64
CAP = 32
REACH = 3
SPAN = 7
NPD = 224
NTILE = 8
TILE = 512
SLABS = 64
YPARTS = 4
NZ = 256
NY = 64
RAYBLOCKS = 4096


def draw_pair_counts(key, part):
    key = jax.random.fold_in(key, 11)
    counts = jax.random.randint(key, (YPARTS, SLABS, SPAN), 1, CAP + 1)
    own = jnp.arange(SPAN) == REACH
    counts = jnp.where(own[None, None, :], CAP, counts)
    dest = jnp.arange(SLABS)[:, None] - REACH + jnp.arange(SPAN)[None, :]
    inside = (dest >= 0) & (dest < SLABS)
    return jnp.where(inside[None, :, :], counts, 0).astype(jnp.int32)


def place_ends(array, own_key, low, high):
    longest = array.shape.index(max(array.shape))
    spots = []
    for shift in (0, 1):
        where = [jax.random.randint(jax.random.fold_in(own_key, axis), (), 0, length) for axis, length in enumerate(array.shape)]
        where[longest] = (where[longest] + shift) % array.shape[longest]
        spots.append(tuple(where))
    return array.at[spots[0]].set(low).at[spots[1]].set(high)


def levels(key, shape, shards, smallest, top_value):
    factor_of = 1.0
    for dim, shards_of in shards:
        steps = jax.random.uniform(jax.random.fold_in(jax.random.fold_in(key, 6), dim), (shards_of,), jnp.float32, smallest / len(shards), top_value / len(shards))
        factor_of = factor_of * jnp.repeat(jnp.exp(steps), shape[dim] // shards_of).reshape((-1,) + (1,) * (len(shape) - 1 - dim))
    return factor_of


def noise(own_key, shape, width, most, pieces=(), kind=jnp.bfloat16):
    loudness = levels(own_key, shape, pieces, -0.22, 0.18) if pieces else 1.0
    values = jax.random.normal(own_key, shape, jnp.float32) * width * loudness
    return jnp.minimum(jnp.maximum(values, -most), most).astype(kind)


def setup_inputs(seed: int = 0) -> dict:
    key_of = jax.random.split(jax.random.key(seed), 10)
    state = noise(key_of[0], (C1, NZ, NY, XD), 1.0, 6.0, ((1, 64), (2, 4)))
    residual = noise(key_of[1], (RAYBLOCKS, ZD, DC), 1.0, 6.0, ((0, 64),))
    projector = noise(key_of[2], (VIEWS, DC, TILE), DC ** -0.5, 0.21875)
    pair_counts = draw_pair_counts(jax.random.fold_in(key_of[9], 71), 0)
    pair_block = place_ends(jax.random.randint(key_of[4], (YPARTS, SLABS, NPD), 0, NBD), jax.random.fold_in(key_of[4], 1), 0, NBD - 1).astype(jnp.int32)
    pair_tile = place_ends(jax.random.randint(key_of[5], (YPARTS, SLABS, NPD), 0, NTILE), jax.random.fold_in(key_of[5], 1), 0, NTILE - 1).astype(jnp.int32)
    pair_view = place_ends(jax.random.randint(key_of[6], (YPARTS, SLABS, NPD), 0, VIEWS), jax.random.fold_in(key_of[6], 1), 0, VIEWS - 1).astype(jnp.int32)
    enc_weight = noise(key_of[7], (2, 2, 2, C2, C1 + 1), (8 * (C1 + 1)) ** -0.5, 0.375)
    dec_weight = noise(key_of[8], (4, 4, 4, C1, C2), (8 * C2) ** -0.5, 0.25)
    return {"state": state, "residual": residual, "projector": projector, "pair_counts": pair_counts, "pair_block": pair_block, "pair_tile": pair_tile, "pair_view": pair_view, "enc_weight": enc_weight, "dec_weight": dec_weight}


def gelu_tanh(values):
    return jax.nn.gelu(values, approximate=True)


def encode(state_part, bproj_part, enc_weight):
    chans, zlen, ylen, xlen = state_part.shape
    zc, yc, xc = zlen // 2, ylen // 2, xlen // 2
    grid = state_part.astype(jnp.float32).reshape(chans, zc, 2, yc, 2, xc, 2)
    extra = bproj_part.astype(jnp.float32).reshape(zc, 2, yc, 2, xc, 2)
    weight = enc_weight.astype(jnp.float32)
    total = jnp.einsum("czaybxe,abeoc->ozyx", grid, weight[..., :chans])
    total = total + jnp.einsum("zaybxe,abeo->ozyx", extra, weight[..., chans])
    return gelu_tanh(total).astype(jnp.bfloat16)


def transposed(coarse, weight):
    chans, zc, yc, xc = coarse.shape
    outc = weight.shape[3]
    planes = []
    for pz in range(2):
        for py in range(2):
            for px in range(2):
                acc = jnp.zeros((outc, zc + 1, yc + 1, xc + 1), jnp.float32)
                for hz in range(2):
                    for hy in range(2):
                        for hx in range(2):
                            term = jnp.einsum("oc,czyx->ozyx", weight[pz + 2 * hz, py + 2 * hy, px + 2 * hx], coarse)
                            acc = acc + jnp.pad(term, ((0, 0), (hz, 1 - hz), (hy, 1 - hy), (hx, 1 - hx)))
                planes.append(acc)
    stacked = jnp.stack(planes).reshape(2, 2, 2, outc, zc + 1, yc + 1, xc + 1)
    return stacked.transpose(3, 4, 0, 5, 1, 6, 2).reshape(outc, 2 * zc + 2, 2 * yc + 2, 2 * xc + 2)


def back_project(residual, projector, pair_counts, pair_block, pair_tile, pair_view):
    ends = jnp.cumsum(pair_counts, axis=-1)
    slots = jnp.arange(NPD, dtype=jnp.int32)
    group = jnp.sum((slots[None, None, :, None] >= ends[:, :, None, :]).astype(jnp.int32), axis=-1)
    valid = group < SPAN
    source = jnp.arange(SLABS, dtype=jnp.int32)[None, :, None]
    dest = jnp.clip(source - REACH + group, 0, SLABS - 1).astype(jnp.int32)
    rays = residual.reshape(SLABS, NBD, ZD, DC)
    proj = projector.astype(jnp.float32).reshape(VIEWS * DC, TILE)
    view_ids = jnp.arange(VIEWS, dtype=jnp.int32)

    def step(acc, index):
        part = index // SLABS
        slab = index % SLABS
        chosen = jnp.take(rays[slab], pair_block[part, slab].astype(jnp.int32), axis=0).astype(jnp.float32)
        onehot = (pair_view[part, slab][:, None] == view_ids[None, :]).astype(jnp.float32)
        spread = chosen[:, :, None, :] * onehot[:, None, :, None]
        contrib = jnp.dot(spread.reshape(NPD * ZD, VIEWS * DC), proj).reshape(NPD, ZD, TILE)
        contrib = jnp.where(valid[part, slab][:, None, None], contrib, 0.0)
        acc = acc.at[part, dest[part, slab], pair_tile[part, slab].astype(jnp.int32)].add(contrib)
        return acc, None

    start = jnp.zeros((YPARTS, SLABS, NTILE, ZD, TILE), jnp.float32)
    total, _ = lax.scan(step, start, jnp.arange(YPARTS * SLABS, dtype=jnp.int32))
    total = total.reshape(YPARTS, SLABS, NTILE, ZD, TY, XD).transpose(1, 3, 0, 2, 4, 5)
    return total.reshape(NZ, NY, XD).astype(jnp.bfloat16)


def reference(state, residual, projector, pair_counts, pair_block, pair_tile, pair_view, enc_weight, dec_weight):
    bproj = back_project(residual, projector, pair_counts, pair_block, pair_tile, pair_view)
    zc = ZD // 2

    def encode_slab(slab):
        part = lax.dynamic_slice_in_dim(state, slab * ZD, ZD, 1)
        extra = lax.dynamic_slice_in_dim(bproj, slab * ZD, ZD, 0)
        return encode(part, extra, enc_weight)

    coarse = lax.map(encode_slab, jnp.arange(SLABS, dtype=jnp.int32))
    coarse = coarse.transpose(1, 0, 2, 3, 4).reshape(C2, NZ // 2, NY // 2, XD // 2)
    padded = jnp.pad(coarse, ((0, 0), (1, 1), (0, 0), (0, 0)))
    dec32 = dec_weight.astype(jnp.float32)

    def decode_slab(slab):
        ext = lax.dynamic_slice_in_dim(padded, slab * zc, zc + 2, 1).astype(jnp.float32)
        fine = transposed(ext, dec32)[:, 3:ZD + 3, 1:NY + 1, 1:XD + 1]
        part = lax.dynamic_slice_in_dim(state, slab * ZD, ZD, 1).astype(jnp.float32)
        return (part + fine).astype(jnp.bfloat16)

    result = lax.map(decode_slab, jnp.arange(SLABS, dtype=jnp.int32))
    return result.transpose(1, 0, 2, 3, 4).reshape(C1, NZ, NY, XD)
```

```python
import jax
import jax.numpy as jnp
from jax import lax
from jax.experimental import pallas as pl
from jax.experimental.pallas import tpu as pltpu
from jax.sharding import PartitionSpec as P

C1, C2 = 32, 64
ZD, YD, XD = 4, 16, 256
XC = XD // 2
SPAN = 7
NPD = 224
VIEWS = 4
NB = 64
DC = 768
TILE = 512
KL = 256
ROWS = 10
NL = ROWS * XC
WIN = 8 * ROWS
MSG = 112
LIST = 256
PAYR = 2 * WIN + 5 * C2
BF, F32, I32 = jnp.bfloat16, jnp.float32, jnp.int32
VLIM = 40 * 1024 * 1024


def dot(a, b):
    return jnp.dot(a, b, preferred_element_type=F32)


def iota(shape, dim):
    return lax.broadcasted_iota(I32, shape, dim)


def split_columns():
    row, col = iota((XD, XD), 0), iota((XD, XD), 1)
    return (row == 2 * (col % XC) + col // XC).astype(BF)


def merge_columns():
    row, col = iota((XD, XD), 0), iota((XD, XD), 1)
    return (col == 2 * (row % XC) + row // XC).astype(BF)


def edge_kernel(counts, block, tile, view, state, idx, up, down, own, lists):
    slab = idx[0]
    split = split_columns()
    row, col = iota((4 * C1, C1 * YD), 0), iota((4 * C1, C1 * YD), 1)
    y = row // C1
    y = jnp.where(y < 2, y, y + YD - 4)
    pick = (col == (row % C1) * YD + y).astype(BF)
    for z in range(ZD):
        plane = state[:, z].reshape(C1 * YD, XD)
        rows = dot(dot(pick, plane).astype(BF), split).astype(BF)
        down[z * 64 : z * 64 + 64, :] = rows[:64]
        up[z * 64 : z * 64 + 64, :] = rows[64:]
    slot = iota((1, NPD), 1)
    group = jnp.zeros((1, NPD), I32)
    end = 0
    for o in range(SPAN):
        end = end + counts[0, slab, o]
        group = group + (slot >= end).astype(I32)
    valid = group < SPAN
    b = block[0, pl.ds(slab, 1), :]
    t = tile[0, pl.ds(slab, 1), :]
    v = view[0, pl.ds(slab, 1), :]
    key = v * NB + b
    own[...] = jnp.full((8, KL), -1, I32)
    own[0:1, :NPD] = key
    own[1:2, :NPD] = jnp.where(valid, group * 16 + t + 1, -1)
    lists[...] = jnp.full((16, KL), -1.0, F32)
    lists[0:1, :NPD] = key.astype(F32)
    lists[1:2, :NPD] = jnp.where(valid & (t == 7), group, -1).astype(F32)
    up[LIST:, :] = lists[...].astype(BF)
    lists[1:2, :NPD] = jnp.where(valid & (t == 0), group, -1).astype(F32)
    down[LIST:, :] = lists[...].astype(BF)


def project_kernel(res, proj, high, low):
    rays = res[...].reshape(4 * NB, DC)
    y = dot(rays, proj[0])
    hi = y.astype(BF)
    lo = (y - hi.astype(F32)).astype(BF)
    for r in range(4):
        high[r] = hi[r * NB : (r + 1) * NB]
        low[r] = lo[r * NB : (r + 1) * NB]


def place_kernel(own, left, right, high, low, idx, mine, up, down, keys):
    part = idx[1]
    keys[0:1, 0:KL] = own[0:1, :].astype(F32)
    keys[1:2, 0:KL] = own[1:2, :].astype(F32)
    lk = left[LIST:, :].astype(F32)
    rk = right[LIST:, :].astype(F32)
    keys[0:1, KL : 2 * KL] = lk[0:1]
    keys[0:1, 2 * KL :] = rk[0:1]
    lg, rg = lk[1:2], rk[1:2]
    keys[1:2, KL : 2 * KL] = jnp.where((lg >= 0) & (part > 0), lg * 16, -1.0)
    keys[1:2, 2 * KL :] = jnp.where((rg >= 0) & (part < 3), rg * 16 + 9, -1.0)
    key = keys[0:1, :].astype(I32)
    skey = keys[1:2, :].astype(I32)
    total = 3 * WIN + 2 * MSG
    row = iota((total, 1), 0)
    inwin = row < 3 * WIN
    w = row // WIN
    k = row % WIN
    n = k // 8
    s = w * 4 - 6 + k % 8
    m = row - 3 * WIN
    isdown = m >= MSG
    mm = jnp.where(isdown, m - MSG, m)
    first = mm < WIN
    mn = jnp.where(first, mm // 8, (mm - WIN) // 2)
    ms_up = jnp.where(first, 6 + mm % 8, 14 + mm % 2)
    ms_dn = jnp.where(first, -10 + mm % 8, -12 + mm % 2)
    n = jnp.where(inwin, n, mn)
    s = jnp.where(inwin, s, jnp.where(isdown, ms_dn, ms_up))
    s = s + 12
    rkey = jnp.where(n < ROWS, (s // 4) * 16 + n, -2)
    r = s % 4
    a = (rkey == skey).astype(BF)
    bk = (iota((VIEWS * NB, 1), 0) == key).astype(BF)
    count = lax.dot_general(a, bk, (((1,), (1,)), ((), ())), preferred_element_type=F32)
    acc = jnp.zeros((total, TILE), F32)
    for q in range(4):
        c = jnp.where(r == q, count, 0.0).astype(BF)
        acc = acc + dot(c, high[q]) + dot(c, low[q])
    mine[...] = acc[: 3 * WIN]
    up[...] = acc[3 * WIN : 3 * WIN + MSG].astype(BF)
    down[...] = acc[3 * WIN + MSG :].astype(BF)


def window_matrix(w, down):
    row, col = iota((WIN, MSG), 0), iota((WIN, MSG), 1)
    n, s = row // 8, 4 * w - 6 + row % 8
    first = col < WIN
    mn = jnp.where(first, col // 8, (col - WIN) // 2)
    if down:
        ms = jnp.where(first, 2 + col % 8, col % 2)
    else:
        ms = jnp.where(first, col % 8 - 6, 2 + col % 2)
    return ((mn == n) & (ms == s)).astype(BF)


def encode_kernel(state, left, right, enc, dec, fs, pre, planes, wdec, x, we):
    split = split_columns()
    row, col = iota((C1 * YD, C1 * YD), 0), iota((C1 * YD, C1 * YD), 1)
    perm = (col == (row % C1) * YD + row // C1).astype(BF)
    for p in range(2):
        for q in range(2):
            for s in range(2):
                k = p * 4 + q * 2 + s
                we[:, k * C1 : (k + 1) * C1] = enc[p, q, s][:, :C1]
    for a in range(2):
        for p in range(2):
            z = 2 * a + p
            plane = state[:, z].reshape(C1 * YD, XD)
            d = dot(dot(perm, plane).astype(BF), split).astype(BF)
            planes[z] = d
            for q in range(2):
                for s in range(2):
                    k = (p * 4 + q * 2 + s) * C1
                    lanes = slice(s * XC, (s + 1) * XC)
                    h = z * 64 + q * C1
                    x[k : k + C1, 0:XC] = left[h : h + C1, lanes]
                    x[k : k + C1, 9 * XC : 10 * XC] = right[h : h + C1, lanes]
                    for b in range(8):
                        y = (2 * b + q) * C1
                        x[k : k + C1, (b + 1) * XC : (b + 2) * XC] = d[y : y + C1, lanes]
        f = dot(we[...], x[...])
        fs[a] = f
        for t in range(5):
            pre[a, t * C2 : (t + 1) * C2, :] = f[:, t * XD : (t + 1) * XD].astype(BF)
    wdec[...] = jnp.zeros_like(wdec)
    taps = (((0, 3), (1, 1)), ((1, 2), (2, 0)))
    for pz in range(2):
        for sel in range(2):
            kz = taps[pz][sel][1]
            for py in range(2):
                for dy, ky in taps[py]:
                    for px in range(2):
                        for dx, kx in taps[px]:
                            r0 = (py * 2 + px) * C1
                            c0 = (sel * 9 + dy * 3 + dx) * C2
                            wdec[pz, r0 : r0 + C1, c0 : c0 + C2] = dec[kz, ky, kx]


def relay_kernel(mine, up, down, pre, pay_up, pay_down):
    for w, pay, plane in ((2, pay_up, 1), (0, pay_down, 0)):
        total = mine[w * WIN : (w + 1) * WIN] + dot(window_matrix(w, False), up[...])
        total = (total + dot(window_matrix(w, True), down[...])).astype(BF)
        pay[0:WIN, :] = total[:, :XD]
        pay[WIN : 2 * WIN, :] = total[:, XD:]
        pay[2 * WIN :, :] = pre[plane]


def decode_kernel(mine, up, down, below, above, fs, planes, wdec, enc, idx, out, bp, x, ns):
    slab, part = idx[0], idx[1]
    split = split_columns()
    merge = merge_columns()
    row, col = iota((C1 * YD, C1 * YD), 0), iota((C1 * YD, C1 * YD), 1)
    perm = (col == (row % YD) * C1 + row // YD).astype(BF)
    centre = mine[WIN : 2 * WIN] + dot(window_matrix(1, False), up[...])
    centre = centre + dot(window_matrix(1, True), down[...])
    for q in range(2):
        rows = slice(q * WIN, (q + 1) * WIN)
        t = centre[:, q * XD : (q + 1) * XD] + below[rows, :].astype(F32) + above[rows, :].astype(F32)
        t = dot(t.astype(BF), split)
        for s in range(2):
            for n in range(ROWS):
                bp[(q * 2 + s) * 8 : (q * 2 + s + 1) * 8, n * XC : (n + 1) * XC] = t[
                    n * 8 : (n + 1) * 8, s * XC : (s + 1) * XC
                ]
    bpb = bp[...].astype(BF)
    lane = iota((C2, XC), 1)
    wlane = iota((C2, 32), 1)
    for a in range(4):
        wb = jnp.zeros((C2, 32), F32)
        for p in range(2):
            for q in range(2):
                for s in range(2):
                    w = enc[p, q, s].astype(F32)[:, C1 : C1 + 1]
                    wb = wb + jnp.where(wlane == (q * 2 + s) * 8 + 2 * a + p, w, 0.0)
        pb = dot(wb.astype(BF), bpb)
        inside = True
        if a == 0:
            inside = slab > 0
        if a == 3:
            inside = slab < 63
        for n in range(ROWS):
            lanes = slice(n * XC, (n + 1) * XC)
            if a in (1, 2):
                v = fs[a - 1, :, lanes]
            else:
                src = below if a == 0 else above
                r0 = 2 * WIN + (n // 2) * C2
                v = src[r0 : r0 + C2, (n % 2) * XC : (n % 2 + 1) * XC].astype(F32)
            v = v + pb[:, lanes]
            v = 0.5 * v * (1.0 + jnp.tanh(0.79788456 * (v + 0.044715 * (v * v * v))))
            ok = inside
            if n == 0:
                ok = (part > 0) & ok
            if n == 9:
                ok = (part < 3) & ok
            if ok is not True:
                v = jnp.where(ok, v, 0.0)
            shifts = (
                jnp.where(lane == 0, 0.0, pltpu.roll(v, 1, 1)).astype(BF),
                v.astype(BF),
                jnp.where(lane == XC - 1, 0.0, pltpu.roll(v, XC - 1, 1)).astype(BF),
            )
            for dy in range(3):
                m = n - dy
                if 0 <= m < 8:
                    for dx in range(3):
                        r0 = a * 576 + dy * 192 + dx * C2
                        x[r0 : r0 + C2, m * XC : (m + 1) * XC] = shifts[dx]
    for f in range(ZD):
        start = (f + 1) // 2 * 576
        d = dot(wdec[f % 2], x[start : start + 1152, :])
        for py in range(2):
            for px in range(2):
                r0 = (py * 2 + px) * C1
                lanes = slice(px * XC, (px + 1) * XC)
                for m in range(8):
                    y = (2 * m + py) * C1
                    old = planes[f, y : y + C1, lanes].astype(F32)
                    ns[y : y + C1, lanes] = (old + d[r0 : r0 + C1, m * XC : (m + 1) * XC]).astype(BF)
        new = dot(dot(perm, ns[...]).astype(BF), merge).astype(BF)
        out[:, f] = new.reshape(C1, YD, XD)


V = pltpu.VMEM
SM = pl.BlockSpec(memory_space=pltpu.SMEM)
VM = pl.BlockSpec(memory_space=pltpu.VMEM)


def shape(dims, dtype=BF):
    return jax.ShapeDtypeStruct(dims, dtype)


def call(kernel, ins, outs, scratch=(), cost=None, vlim=VLIM, **more):
    return pl.pallas_call(
        kernel,
        in_specs=ins,
        out_specs=[VM] * len(outs) if "grid" not in more else more.pop("specs"),
        out_shape=outs,
        scratch_shapes=scratch,
        compiler_params=pltpu.CompilerParams(vmem_limit_bytes=vlim),
        cost_estimate=cost,
        **more,
    )


def cost(us):
    return pl.CostEstimate(flops=int(us * 1e9), bytes_accessed=int(us * 3e6), transcendentals=0)


def shifted(block, axis, distance):
    n = lax.axis_size(axis)
    return lax.ppermute(block, axis, [(i, (i + distance) % n) for i in range(n)])


def per_device(
    state, residual, projector, pair_counts, pair_block, pair_tile, pair_view, enc_weight, dec_weight
):
    idx = jnp.stack([lax.axis_index("gz"), lax.axis_index("gy")]).astype(I32)
    up, down, own = call(
        edge_kernel,
        [SM, VM, VM, VM, VM, SM],
        [shape((272, XD)), shape((272, XD)), shape((8, KL), I32)],
        [V((16, KL), F32)],
        cost=cost(1.0),
        name="edge",
    )(pair_counts, pair_block, pair_tile, pair_view, state, idx)
    left = shifted(up, "gy", 1)
    right = shifted(down, "gy", -1)
    rays = jnp.transpose(residual, (1, 0, 2))
    high, low = call(
        project_kernel,
        [
            pl.BlockSpec((4, NB, DC), lambda v: (0, 0, 0)),
            pl.BlockSpec((1, DC, TILE), lambda v: (v, 0, 0)),
        ],
        [shape((4, VIEWS * NB, TILE)), shape((4, VIEWS * NB, TILE))],
        cost=cost(3.0),
        grid=(VIEWS,),
        specs=[pl.BlockSpec((4, NB, TILE), lambda v: (0, v, 0))] * 2,
        name="project",
    )(rays, projector)
    mine, msg_up, msg_down = call(
        place_kernel,
        [VM, VM, VM, VM, VM, SM],
        [shape((3 * WIN, TILE), F32), shape((MSG, TILE)), shape((MSG, TILE))],
        [V((8, 3 * KL), F32)],
        cost=cost(2.0),
        name="place",
    )(own, left, right, high, low, idx)
    got_up = shifted(msg_up, "gz", 3)
    got_down = shifted(msg_down, "gz", -3)
    fs, pre, planes, wdec = call(
        encode_kernel,
        [VM] * 5,
        [
            shape((2, C2, NL), F32),
            shape((2, 5 * C2, XD)),
            shape((ZD, C1 * YD, XD)),
            shape((2, 128, 1152)),
        ],
        [V((8 * C1, NL), BF), V((C2, 8 * C1), BF)],
        cost=cost(4.0),
        name="encode",
    )(state, left, right, enc_weight, dec_weight)
    pay_up, pay_down = call(
        relay_kernel,
        [VM] * 4,
        [shape((PAYR, XD)), shape((PAYR, XD))],
        cost=cost(1.0),
        name="relay",
    )(mine, got_up, got_down, pre)
    below = shifted(pay_up, "gz", 1)
    above = shifted(pay_down, "gz", -1)
    return call(
        decode_kernel,
        [VM] * 9 + [SM],
        [shape((C1, ZD, YD, XD))],
        [V((32, NL), F32), V((2304, 8 * XC), BF), V((C1 * YD, XD), BF)],
        cost=cost(6.0),
        name="decode",
    )(mine, got_up, got_down, below, above, fs, planes, wdec, enc_weight, idx)[0]


def solution(mesh):
    in_specs = (
        P(None, "gz", "gy", None),
        P("gz", None, None),
        P(),
        P("gy", None, None),
        P("gy", None, None),
        P("gy", None, None),
        P("gy", None, None),
        P(),
        P(),
    )
    out_specs = P(None, "gz", "gy", None)
    return jax.shard_map(
        per_device, mesh=mesh, in_specs=in_specs, out_specs=out_specs, check_vma=False
    )
```

```python
import jax
import jax.numpy as jnp
from jax import lax
from jax.experimental import pallas as pl
from jax.experimental.pallas import tpu as pltpu
from jax.sharding import PartitionSpec as P

C1, C2 = 32, 64
ZD, YD, XD = 4, 16, 256
XC = XD // 2
SPAN = 7
NPD = 224
VIEWS = 4
NB = 64
DC = 768
TILE = 512
KL = 256
ROWS = 10
NL = ROWS * XC
CHIP = 12 * ROWS
OWN = 8 * ROWS
FAR = 6 * ROWS
MATE = 10 * ROWS
LIST = 256
BF, F32, I32 = jnp.bfloat16, jnp.float32, jnp.int32
MIB = 1024 * 1024


def dot(a, b):
    return jnp.dot(a, b, preferred_element_type=F32)


def iota(shape, dim):
    return lax.broadcasted_iota(I32, shape, dim)


def split_columns():
    row, col = iota((XD, XD), 0), iota((XD, XD), 1)
    return (row == 2 * (col % XC) + col // XC).astype(BF)


def merge_columns():
    row, col = iota((XD, XD), 0), iota((XD, XD), 1)
    return (col == 2 * (row % XC) + row // XC).astype(BF)


def edge_kernel(counts, block, tile, view, state, idx, up, down, own, lists, cs, pairs, planes, sems):
    slab = idx[0]
    at = pl.multiple_of((slab // 8) * 8, 8)
    copies = [pltpu.make_async_copy(counts, cs, sems.at[0])]
    for i, ref in enumerate((block, tile, view)):
        copies.append(pltpu.make_async_copy(ref.at[0, pl.ds(at, 8)], pairs.at[i], sems.at[1 + i]))
    for z in range(ZD):
        copies.append(pltpu.make_async_copy(state.at[:, z], planes.at[z], sems.at[4 + z]))
    for copy in copies:
        copy.start()
    split = split_columns()
    row, col = iota((4 * C1, C1 * YD), 0), iota((4 * C1, C1 * YD), 1)
    y = row // C1
    y = jnp.where(y < 2, y, y + YD - 4)
    pick = (col == (row % C1) * YD + y).astype(BF)
    lists[...] = jnp.full((16, KL), -1.0, F32)
    own[...] = jnp.full((8, KL), -1, I32)
    for copy in copies[:4]:
        copy.wait()
    slot = iota((1, NPD), 1)
    group = jnp.zeros((1, NPD), I32)
    end = 0
    for o in range(SPAN):
        end = end + cs[o, 0, slab]
        group = group + (slot >= end).astype(I32)
    valid = group < SPAN
    rest = pl.ds(slab % 8, 1)
    b, t, v = pairs[0, rest, :], pairs[1, rest, :], pairs[2, rest, :]
    key = v * NB + b
    own[0:1, :NPD] = key
    own[1:2, :NPD] = jnp.where(valid, group * 16 + t + 1, -1)
    lists[0:1, :NPD] = key.astype(F32)
    lists[1:2, :NPD] = jnp.where(valid & (t == 7), group, -1).astype(F32)
    up[LIST:, :] = lists[...].astype(BF)
    lists[1:2, :NPD] = jnp.where(valid & (t == 0), group, -1).astype(F32)
    down[LIST:, :] = lists[...].astype(BF)
    for z in range(ZD):
        copies[4 + z].wait()
        rows = dot(dot(pick, planes[z].reshape(C1 * YD, XD)).astype(BF), split).astype(BF)
        down[z * 64 : z * 64 + 64, :] = rows[:64]
        up[z * 64 : z * 64 + 64, :] = rows[64:]


def project_kernel(res, proj, high, low):
    rays = res[...].reshape(4 * NB, DC)
    y = dot(rays, proj[0])
    hi = y.astype(BF)
    lo = (y - hi.astype(F32)).astype(BF)
    for r in range(4):
        high[r] = hi[r * NB : (r + 1) * NB]
        low[r] = lo[r * NB : (r + 1) * NB]


def place_kernel(own, left, right, high, low, we, idx, win, near, far, mate, fh, keys, x):
    slab, part = idx[0], idx[1]
    core = slab % 2
    keys[0:1, 0:KL] = own[0:1, :].astype(F32)
    keys[1:2, 0:KL] = own[1:2, :].astype(F32)
    lk = left[LIST:, :].astype(F32)
    rk = right[LIST:, :].astype(F32)
    keys[0:1, KL : 2 * KL] = lk[0:1]
    keys[0:1, 2 * KL :] = rk[0:1]
    lg, rg = lk[1:2], rk[1:2]
    keys[1:2, KL : 2 * KL] = jnp.where((lg >= 0) & (part > 0), lg * 16, -1.0)
    keys[1:2, 2 * KL :] = jnp.where((rg >= 0) & (part < 3), rg * 16 + 9, -1.0)
    key = keys[0:1, :].astype(I32)
    skey = keys[1:2, :].astype(I32)
    total = 416
    row = iota((total, 1), 0)

    def pieces(values):
        w, n, m, f = values
        return jnp.where(row < 120, w, jnp.where(row < 240, n, jnp.where(row < 352, m, f)))

    k = row - pieces((0, 120, 240, 352))
    t = k // ROWS
    n = k % ROWS
    even = core == 0
    first = jnp.where(even, pieces((-2, 1, 6, -7)), pieces((5, 2, -3, 10)))
    step = jnp.where(even, pieces((1, -1, 1, -1)), pieces((-1, 1, -1, 1)))
    s = first + step * t + 12
    rkey = jnp.where(t < pieces((12, 12, 10, 6)), (s // 4) * 16 + n, -2)
    r = s % 4
    a = (rkey == skey).astype(BF)
    bk = (iota((VIEWS * NB, 1), 0) == key).astype(BF)
    count = lax.dot_general(a, bk, (((1,), (1,)), ((), ())), preferred_element_type=F32)
    acc = jnp.zeros((total, TILE), F32)
    for q in range(4):
        c = jnp.where(r == q, count, 0.0).astype(BF)
        acc = acc + dot(c, high[q]) + dot(c, low[q])
    win[...] = acc[:120]
    near[...] = acc[120:240]
    mate[...] = acc[240:352].astype(BF)
    far[...] = acc[352:]
    for a in range(2):
        for p in range(2):
            for q in range(2):
                for s in range(2):
                    k = (p * 4 + q * 2 + s) * C1
                    lanes = slice(s * XC, (s + 1) * XC)
                    h = (2 * a + p) * 64 + q * C1
                    x[k : k + C1, 2 * a * XC : (2 * a + 1) * XC] = left[h : h + C1, lanes]
                    x[k : k + C1, (2 * a + 1) * XC : (2 * a + 2) * XC] = right[h : h + C1, lanes]
    f = lax.dot_general(we[...], x[...], (((0,), (0,)), ((), ())), preferred_element_type=F32)
    fh[0] = f[:, :XD]
    fh[1] = f[:, XD:]


def encode_kernel(state, enc, fs, planes, we, wb, x):
    split = split_columns()
    row, col = iota((C1 * YD, C1 * YD), 0), iota((C1 * YD, C1 * YD), 1)
    perm = (col == (row % C1) * YD + row // C1).astype(BF)
    rows = iota((32, C2), 0)
    bias = [jnp.zeros((32, C2), F32) for _ in range(4)]
    for p in range(2):
        for q in range(2):
            e = enc[p, q].astype(F32)
            for s in range(2):
                k = p * 4 + q * 2 + s
                es = e[:, s, :]
                we[k * C1 : (k + 1) * C1, :] = es[:C1].astype(BF)
                for a in range(4):
                    bias[a] = bias[a] + jnp.where(rows == (q * 2 + s) * 8 + 2 * a + p, es[C1 : C1 + 1], 0.0)
    for a in range(4):
        wb[a] = bias[a].astype(BF)
    for a in range(2):
        for p in range(2):
            z = 2 * a + p
            plane = state[:, z].reshape(C1 * YD, XD)
            d = dot(dot(perm, plane).astype(BF), split).astype(BF)
            planes[z] = d
            for q in range(2):
                for s in range(2):
                    k = (p * 4 + q * 2 + s) * C1
                    for b in range(8):
                        y = (2 * b + q) * C1
                        x[k : k + C1, b * XC : (b + 1) * XC] = d[y : y + C1, s * XC : (s + 1) * XC]
        fs[a] = lax.dot_general(we[...], x[...], (((0,), (0,)), ((), ())), preferred_element_type=F32)


def weights_kernel(dec, wdec):
    wdec[...] = jnp.zeros_like(wdec)
    taps = (((0, 3), (1, 1)), ((1, 2), (2, 0)))
    for pz in range(2):
        for sel in range(2):
            kz = taps[pz][sel][1]
            for py in range(2):
                for dy, ky in taps[py]:
                    for px in range(2):
                        for dx, kx in taps[px]:
                            r0 = (py * 2 + px) * C1
                            c0 = (sel * 9 + dy * 3 + dx) * C2
                            wdec[pz, r0 : r0 + C1, c0 : c0 + C2] = dec[kz, ky, kx]


def put_plane(pay, start, fs, fh, plane):
    for n in range(ROWS):
        if n == 0:
            f = fh[plane, :, :XC]
        elif n == 9:
            f = fh[plane, :, XC:]
        else:
            f = fs[plane, :, (n - 1) * XC : n * XC]
        r0 = start + (n // 2) * C2
        pay[r0 : r0 + C2, (n % 2) * XC : (n % 2 + 1) * XC] = f.astype(BF)


def out_kernel(near, far, got, fs, fh, idx, pay, pay_far, tmp):
    tmp[0:CHIP] = near[...]
    tmp[CHIP:128] = jnp.zeros((8, TILE), F32)
    tmp[0:MATE] += got[...].astype(F32)[:MATE]
    total = tmp[...].astype(BF)
    pay[0:128, :] = total[:, :XD]
    pay[128:256, :] = total[:, XD:]
    tmp[0:64] = far[...]
    tmp[0 : 2 * ROWS] += got[...].astype(F32)[8 * ROWS : MATE]
    pay_far[...] = tmp[0:64].astype(BF)
    put_plane(pay, 256, fs, fh, idx[0] % 2)


def window(win, near, far):
    left = win[:, :XD] + near[0:128, :].astype(F32)[:CHIP]
    right = win[:, XD:] + near[128:256, :].astype(F32)[:CHIP]
    return left, right, far[...].astype(F32)


def mate_kernel(win, near, far, fs, fh, idx, pay, tmp):
    for q, half in enumerate(window(win, near, far)[:2]):
        tmp[...] = half
        tmp[0:64] += far[:, q * XD : (q + 1) * XD].astype(F32)
        pay[q * OWN : (q + 1) * OWN, :] = tmp[CHIP - OWN :, :].astype(BF)
    put_plane(pay, 2 * OWN, fs, fh, 1 - idx[0] % 2)


def decode_kernel(win, near, far, mate, fs, fh, planes, wdec, wb, idx, out, bp, x, ns, tmp):
    slab, part = idx[0], idx[1]
    core = slab % 2
    split = split_columns()
    merge = merge_columns()
    row, col = iota((C1 * YD, C1 * YD), 0), iota((C1 * YD, C1 * YD), 1)
    perm = (col == (row % YD) * C1 + row // YD).astype(BF)
    row, col = iota((OWN, OWN), 0), iota((OWN, OWN), 1)
    turn = ((col % ROWS == row % ROWS) & (col // ROWS == 7 - row // ROWS)).astype(BF)
    z = row % 8
    z = jnp.where(core == 0, z, 7 - z)
    sort = ((col % ROWS == row // 8) & (col // ROWS == z)).astype(BF)
    for q, half in enumerate(window(win, near, far)[:2]):
        tmp[...] = half
        tmp[0:64] += far[:, q * XD : (q + 1) * XD].astype(F32)
        t = tmp[0:OWN] + dot(turn, mate[q * OWN : (q + 1) * OWN, :])
        t = dot(dot(sort, t.astype(BF)).astype(BF), split)
        for s in range(2):
            for n in range(ROWS):
                bp[(q * 2 + s) * 8 : (q * 2 + s + 1) * 8, n * XC : (n + 1) * XC] = t[
                    n * 8 : (n + 1) * 8, s * XC : (s + 1) * XC
                ]
    bpb = bp[...].astype(BF)
    lane = iota((C2, XC), 1)
    for a in range(4):
        pb = lax.dot_general(wb[a], bpb, (((0,), (0,)), ((), ())), preferred_element_type=F32)
        inside = True
        if a == 0:
            inside = slab > 0
        if a == 3:
            inside = slab < 63
        for n in range(ROWS):
            lanes = slice(n * XC, (n + 1) * XC)
            if a in (1, 2):
                if n == 0:
                    v = fh[a - 1, :, :XC]
                elif n == 9:
                    v = fh[a - 1, :, XC:]
                else:
                    v = fs[a - 1, :, (n - 1) * XC : n * XC]
            else:
                half = slice((n % 2) * XC, (n % 2 + 1) * XC)
                r0 = (n // 2) * C2
                v1 = near[256 + r0 : 256 + r0 + C2, half].astype(F32)
                v2 = mate[2 * OWN + r0 : 2 * OWN + r0 + C2, half].astype(F32)
                v = jnp.where(core == (0 if a == 0 else 1), v1, v2)
            v = v + pb[:, lanes]
            v = 0.5 * v * (1.0 + jnp.tanh(0.79788456 * (v + 0.044715 * (v * v * v))))
            ok = inside
            if n == 0:
                ok = (part > 0) & ok
            if n == 9:
                ok = (part < 3) & ok
            if ok is not True:
                v = jnp.where(ok, v, 0.0)
            shifts = (
                jnp.where(lane == 0, 0.0, pltpu.roll(v, 1, 1)).astype(BF),
                v.astype(BF),
                jnp.where(lane == XC - 1, 0.0, pltpu.roll(v, XC - 1, 1)).astype(BF),
            )
            for dy in range(3):
                m = n - dy
                if 0 <= m < 8:
                    for dx in range(3):
                        r0 = a * 576 + dy * 192 + dx * C2
                        x[r0 : r0 + C2, m * XC : (m + 1) * XC] = shifts[dx]
    for f in range(ZD):
        start = (f + 1) // 2 * 576
        d = dot(wdec[f % 2], x[start : start + 1152, :])
        for py in range(2):
            for px in range(2):
                r0 = (py * 2 + px) * C1
                lanes = slice(px * XC, (px + 1) * XC)
                for m in range(8):
                    y = (2 * m + py) * C1
                    old = planes[f, y : y + C1, lanes].astype(F32)
                    ns[y : y + C1, lanes] = (old + d[r0 : r0 + C1, m * XC : (m + 1) * XC]).astype(BF)
        new = dot(dot(perm, ns[...]).astype(BF), merge).astype(BF)
        out[:, f] = new.reshape(C1, YD, XD)


V = pltpu.VMEM
SM = pl.BlockSpec(memory_space=pltpu.SMEM)
VM = pl.BlockSpec(memory_space=pltpu.VMEM)
ANY = pl.BlockSpec(memory_space=pl.ANY)


def shape(dims, dtype=BF):
    return jax.ShapeDtypeStruct(dims, dtype)


def call(kernel, ins, outs, scratch=(), cost=None, vlim=16 * MIB, **more):
    return pl.pallas_call(
        kernel,
        in_specs=ins,
        out_specs=[VM] * len(outs) if "grid" not in more else more.pop("specs"),
        out_shape=outs,
        scratch_shapes=scratch,
        compiler_params=pltpu.CompilerParams(vmem_limit_bytes=vlim),
        cost_estimate=cost,
        **more,
    )


def cost(us):
    return pl.CostEstimate(flops=int(us * 1e9), bytes_accessed=int(us * 3e6), transcendentals=0)


def shifted(block, axis, distance):
    n = lax.axis_size(axis)
    return lax.ppermute(block, axis, [(i, (i + distance) % n) for i in range(n)])


def swapped(block, distance):
    n = lax.axis_size("gz")
    route = []
    for i in range(0, n, 2):
        j = (i + distance) % n
        route += [(i, j), (j, i)]
    return lax.ppermute(block, "gz", route)


def per_device(
    state, residual, projector, pair_counts, pair_block, pair_tile, pair_view, enc_weight, dec_weight
):
    idx = jnp.stack([lax.axis_index("gz"), lax.axis_index("gy")]).astype(I32)
    up, down, own = call(
        edge_kernel,
        [ANY] * 5 + [SM],
        [shape((272, XD)), shape((272, XD)), shape((8, KL), I32)],
        [
            V((16, KL), F32),
            pltpu.SMEM((SPAN, 1, 64), I32),
            V((3, 8, NPD), I32),
            V((ZD, C1, YD, XD), BF),
            pltpu.SemaphoreType.DMA((8,)),
        ],
        cost=cost(1.0),
        vlim=56 * MIB,
        name="edge",
    )(jnp.transpose(pair_counts, (2, 0, 1)), pair_block, pair_tile, pair_view, state, idx)
    left = shifted(up, "gy", 1)
    right = shifted(down, "gy", -1)
    rays = jnp.transpose(residual, (1, 0, 2))
    high, low = call(
        project_kernel,
        [
            pl.BlockSpec((4, NB, DC), lambda v: (0, 0, 0)),
            pl.BlockSpec((1, DC, TILE), lambda v: (v, 0, 0)),
        ],
        [shape((4, VIEWS * NB, TILE)), shape((4, VIEWS * NB, TILE))],
        cost=cost(2.0),
        grid=(VIEWS,),
        specs=[pl.BlockSpec((4, NB, TILE), lambda v: (0, v, 0))] * 2,
        name="project",
    )(rays, projector)
    fs, planes, we, wb = call(
        encode_kernel,
        [VM] * 2,
        [
            shape((2, C2, 8 * XC), F32),
            shape((ZD, C1 * YD, XD)),
            shape((8 * C1, C2)),
            shape((4, 32, C2)),
        ],
        [V((8 * C1, 8 * XC), BF)],
        cost=cost(2.0),
        name="encode",
    )(state, jnp.transpose(enc_weight, (0, 1, 4, 2, 3)))
    win, near, far, mate, fh = call(
        place_kernel,
        [VM] * 6 + [SM],
        [
            shape((CHIP, TILE), F32),
            shape((CHIP, TILE), F32),
            shape((64, TILE), F32),
            shape((112, TILE)),
            shape((2, C2, XD), F32),
        ],
        [V((8, 3 * KL), F32), V((8 * C1, 4 * XC), BF)],
        cost=cost(2.5),
        name="place",
    )(own, left, right, high, low, we, idx)
    got = swapped(mate, 1)
    pay, pay_far = call(
        out_kernel,
        [VM] * 5 + [SM],
        [shape((576, XD)), shape((64, TILE))],
        [V((128, TILE), F32)],
        cost=cost(0.4),
        name="outward",
    )(near, far, got, fs, fh, idx)
    got_near = swapped(pay, -1)
    got_far = swapped(pay_far, -3)
    wdec = call(
        weights_kernel, [VM], [shape((2, 128, 1152))], cost=cost(3.0), name="weights"
    )(dec_weight)[0]
    pay_mate = call(
        mate_kernel,
        [VM] * 5 + [SM],
        [shape((2 * OWN + 5 * C2, XD))],
        [V((CHIP, XD), F32)],
        cost=cost(0.4),
        name="inward",
    )(win, got_near, got_far, fs, fh, idx)[0]
    got_mate = swapped(pay_mate, 1)
    return call(
        decode_kernel,
        [VM] * 9 + [SM],
        [shape((C1, ZD, YD, XD))],
        [V((32, NL), F32), V((2304, 8 * XC), BF), V((C1 * YD, XD), BF), V((CHIP, XD), F32)],
        cost=cost(6.0),
        vlim=24 * MIB,
        name="decode",
    )(win, got_near, got_far, got_mate, fs, fh, planes, wdec, wb, idx)[0]


def solution(mesh):
    in_specs = (
        P(None, "gz", "gy", None),
        P("gz", None, None),
        P(),
        P("gy", None, None),
        P("gy", None, None),
        P("gy", None, None),
        P("gy", None, None),
        P(),
        P(),
    )
    out_specs = P(None, "gz", "gy", None)
    return jax.shard_map(
        per_device, mesh=mesh, in_specs=in_specs, out_specs=out_specs, check_vma=False
    )
```

```python
import jax
import jax.numpy as jnp
from jax import lax
from jax.experimental import pallas as pl
from jax.experimental.pallas import tpu as pltpu
from jax.sharding import PartitionSpec as P

C1, C2 = 32, 64
ZD, YD, XD = 4, 16, 256
XC = XD // 2
SPAN = 7
NPD = 224
VIEWS = 4
NB = 64
DC = 768
TILE = 512
KL = 256
ROWS = 10
NL = ROWS * XC
CHIP = 12 * ROWS
OWN = 8 * ROWS
FAR = 6 * ROWS
MATE = 10 * ROWS
LIST = 256
BF, F32, I32 = jnp.bfloat16, jnp.float32, jnp.int32
MIB = 1024 * 1024


def dot(a, b):
    return jnp.dot(a, b, preferred_element_type=F32)


def iota(shape, dim):
    return lax.broadcasted_iota(I32, shape, dim)


def split_columns():
    row, col = iota((XD, XD), 0), iota((XD, XD), 1)
    return (row == 2 * (col % XC) + col // XC).astype(BF)


def merge_columns():
    row, col = iota((XD, XD), 0), iota((XD, XD), 1)
    return (col == 2 * (row % XC) + row // XC).astype(BF)


def edge_kernel(counts, block, tile, view, state, up, down, own, lists, cs, pairs, planes, some, sems):
    slab = lax.axis_index("gz")
    at = pl.multiple_of((slab // 8) * 8, 8)
    copies = [pltpu.make_async_copy(counts, cs, sems.at[0])]
    for i, ref in enumerate((block, tile, view)):
        copies.append(pltpu.make_async_copy(ref.at[0, pl.ds(at, 8)], pairs.at[i], sems.at[1 + i]))
    for z in range(ZD):
        copies.append(pltpu.make_async_copy(state.at[:, z], planes.at[z], sems.at[4 + z]))
    for copy in copies:
        copy.start()
    split = split_columns()
    row, col = iota((4 * C1, C1 * YD), 0), iota((4 * C1, C1 * YD), 1)
    y = row // C1
    y = jnp.where(y < 2, y, y + YD - 4)
    pick = (col == (row % C1) * YD + y).astype(BF)
    lists[...] = jnp.full((16, KL), -1.0, F32)
    own[...] = jnp.full((8, KL), -1, I32)
    for copy in copies[:4]:
        copy.wait()
    slot = iota((1, NPD), 1)
    group = jnp.zeros((1, NPD), I32)
    end = 0
    for o in range(SPAN):
        end = end + cs[o, 0, slab]
        group = group + (slot >= end).astype(I32)
    valid = group < SPAN
    rest = pl.ds(slab % 8, 1)
    b, t, v = pairs[0, rest, :], pairs[1, rest, :], pairs[2, rest, :]
    key = v * NB + b
    own[0:1, :NPD] = key
    own[1:2, :NPD] = jnp.where(valid, group * 16 + t + 1, -1)
    lists[0:1, :NPD] = key.astype(F32)
    lists[1:2, :NPD] = jnp.where(valid & (t == 7), group, -1).astype(F32)
    up[LIST:, :] = lists[...].astype(BF)
    lists[1:2, :NPD] = jnp.where(valid & (t == 0), group, -1).astype(F32)
    down[LIST:, :] = lists[...].astype(BF)
    for z in range(ZD):
        copies[4 + z].wait()
        some[z * 128 : (z + 1) * 128, :] = dot(pick, planes[z].reshape(C1 * YD, XD)).astype(BF)
    rows = dot(some[...], split).astype(BF)
    for z in range(ZD):
        down[z * 64 : z * 64 + 64, :] = rows[z * 128 : z * 128 + 64]
        up[z * 64 : z * 64 + 64, :] = rows[z * 128 + 64 : z * 128 + 128]


def project_kernel(res, proj, high, low):
    rays = res[...].reshape(4 * NB, DC)
    y = dot(rays, proj[0])
    hi = y.astype(BF)
    lo = (y - hi.astype(F32)).astype(BF)
    for r in range(4):
        high[r] = hi[r * NB : (r + 1) * NB]
        low[r] = lo[r * NB : (r + 1) * NB]


def place_kernel(own, left, right, high, low, we, win, near, far, mate, fh, keys, x):
    slab, part = lax.axis_index("gz"), lax.axis_index("gy")
    core = slab % 2
    keys[0:1, 0:KL] = own[0:1, :].astype(F32)
    keys[1:2, 0:KL] = own[1:2, :].astype(F32)
    lk = left[LIST:, :].astype(F32)
    rk = right[LIST:, :].astype(F32)
    keys[0:1, KL : 2 * KL] = lk[0:1]
    keys[0:1, 2 * KL :] = rk[0:1]
    lg, rg = lk[1:2], rk[1:2]
    keys[1:2, KL : 2 * KL] = jnp.where((lg >= 0) & (part > 0), lg * 16, -1.0)
    keys[1:2, 2 * KL :] = jnp.where((rg >= 0) & (part < 3), rg * 16 + 9, -1.0)
    key = keys[0:1, :].astype(I32)
    skey = keys[1:2, :].astype(I32)
    total = 416
    row = iota((total, 1), 0)

    def pieces(values):
        w, n, m, f = values
        return jnp.where(row < 120, w, jnp.where(row < 240, n, jnp.where(row < 352, m, f)))

    k = row - pieces((0, 120, 240, 352))
    t = k // ROWS
    n = k % ROWS
    even = core == 0
    first = jnp.where(even, pieces((-2, 1, 6, -7)), pieces((5, 2, -3, 10)))
    step = jnp.where(even, pieces((1, -1, 1, -1)), pieces((-1, 1, -1, 1)))
    s = first + step * t + 12
    rkey = jnp.where(t < pieces((12, 12, 10, 6)), (s // 4) * 16 + n, -2)
    r = s % 4
    a = (rkey == skey).astype(BF)
    bk = (iota((VIEWS * NB, 1), 0) == key).astype(BF)
    count = lax.dot_general(a, bk, (((1,), (1,)), ((), ())), preferred_element_type=F32)
    each = jnp.concatenate([jnp.where(r == q, count, 0.0).astype(BF) for q in range(4)], axis=1)
    acc = dot(each, high[...].reshape(4 * VIEWS * NB, TILE)) + dot(each, low[...].reshape(4 * VIEWS * NB, TILE))
    win[...] = acc[:120]
    near[...] = acc[120:240]
    mate[...] = acc[240:352].astype(BF)
    far[...] = acc[352:]
    for a in range(2):
        for p in range(2):
            for q in range(2):
                for s in range(2):
                    k = (p * 4 + q * 2 + s) * C1
                    lanes = slice(s * XC, (s + 1) * XC)
                    h = (2 * a + p) * 64 + q * C1
                    x[k : k + C1, 2 * a * XC : (2 * a + 1) * XC] = left[h : h + C1, lanes]
                    x[k : k + C1, (2 * a + 1) * XC : (2 * a + 2) * XC] = right[h : h + C1, lanes]
    f = lax.dot_general(we[...], x[...], (((0,), (0,)), ((), ())), preferred_element_type=F32)
    fh[0] = f[:, :XD]
    fh[1] = f[:, XD:]


def encode_kernel(state, enc, fs, planes, we, wb, x):
    split = split_columns()
    row, col = iota((C1 * YD, C1 * YD), 0), iota((C1 * YD, C1 * YD), 1)
    perm = (col == (row % C1) * YD + row // C1).astype(BF)
    rows = iota((32, C2), 0)
    bias = [jnp.zeros((32, C2), F32) for _ in range(4)]
    for p in range(2):
        for q in range(2):
            e = enc[p, q].astype(F32)
            for s in range(2):
                k = p * 4 + q * 2 + s
                es = e[:, s, :]
                we[k * C1 : (k + 1) * C1, :] = es[:C1].astype(BF)
                for a in range(4):
                    bias[a] = bias[a] + jnp.where(rows == (q * 2 + s) * 8 + 2 * a + p, es[C1 : C1 + 1], 0.0)
    for a in range(4):
        wb[a] = bias[a].astype(BF)
    for a in range(2):
        for p in range(2):
            z = 2 * a + p
            plane = state[:, z].reshape(C1 * YD, XD)
            d = dot(dot(perm, plane).astype(BF), split).astype(BF)
            planes[z] = d
            for q in range(2):
                for s in range(2):
                    k = (p * 4 + q * 2 + s) * C1
                    for b in range(8):
                        y = (2 * b + q) * C1
                        x[k : k + C1, b * XC : (b + 1) * XC] = d[y : y + C1, s * XC : (s + 1) * XC]
        fs[a] = lax.dot_general(we[...], x[...], (((0,), (0,)), ((), ())), preferred_element_type=F32)


def prepare_kernel(dec, wdec, mats, small):
    mats[0:XD, 0:XD] = split_columns()
    mats[0:XD, XD : 2 * XD] = merge_columns()
    row, col = iota((C1 * YD, C1 * YD), 0), iota((C1 * YD, C1 * YD), 1)
    mats[XD:, :] = (col == (row % YD) * C1 + row // YD).astype(BF)
    core = lax.axis_index("gz") % 2
    row, col = iota((OWN, OWN), 0), iota((OWN, OWN), 1)
    small[0] = ((col % ROWS == row % ROWS) & (col // ROWS == 7 - row // ROWS)).astype(BF)
    z = row % 8
    z = jnp.where(core == 0, z, 7 - z)
    small[1] = ((col % ROWS == row // 8) & (col // ROWS == z)).astype(BF)
    wdec[...] = jnp.zeros_like(wdec)
    taps = (((0, 3), (1, 1)), ((1, 2), (2, 0)))
    for pz in range(2):
        for sel in range(2):
            kz = taps[pz][sel][1]
            for py in range(2):
                for dy, ky in taps[py]:
                    for px in range(2):
                        for dx, kx in taps[px]:
                            r0 = (py * 2 + px) * C1
                            c0 = (sel * 9 + dy * 3 + dx) * C2
                            wdec[pz, r0 : r0 + C1, c0 : c0 + C2] = dec[kz, ky, kx]


def put_plane(pay, start, fs, fh, plane):
    for n in range(ROWS):
        if n == 0:
            f = fh[plane, :, :XC]
        elif n == 9:
            f = fh[plane, :, XC:]
        else:
            f = fs[plane, :, (n - 1) * XC : n * XC]
        r0 = start + (n // 2) * C2
        pay[r0 : r0 + C2, (n % 2) * XC : (n % 2 + 1) * XC] = f.astype(BF)


def out_kernel(near, far, got, fs, fh, pay, pay_far, tmp):
    tmp[0:CHIP] = near[...]
    tmp[CHIP:128] = jnp.zeros((8, TILE), F32)
    tmp[0:MATE] += got[...].astype(F32)[:MATE]
    total = tmp[...].astype(BF)
    pay[0:128, :] = total[:, :XD]
    pay[128:256, :] = total[:, XD:]
    tmp[0:64] = far[...]
    tmp[0 : 2 * ROWS] += got[...].astype(F32)[8 * ROWS : MATE]
    pay_far[...] = tmp[0:64].astype(BF)
    put_plane(pay, 256, fs, fh, lax.axis_index("gz") % 2)


def window(win, near, far):
    left = win[:, :XD] + near[0:128, :].astype(F32)[:CHIP]
    right = win[:, XD:] + near[128:256, :].astype(F32)[:CHIP]
    return left, right, far[...].astype(F32)


def mate_kernel(win, near, far, fs, fh, mats, pay, tmp):
    for q, half in enumerate(window(win, near, far)[:2]):
        tmp[...] = half
        tmp[0:64] += far[:, q * XD : (q + 1) * XD].astype(F32)
        pay[q * OWN : (q + 1) * OWN, :] = tmp[CHIP - OWN :, :].astype(BF)
    put_plane(pay, 2 * OWN, fs, fh, 1 - lax.axis_index("gz") % 2)


def decode_kernel(win, near, far, mate, fs, fh, planes, wdec, wb, mats, small, out, bp, x, ns, tmp, stage, sems):
    slab, part = lax.axis_index("gz"), lax.axis_index("gy")
    core = slab % 2
    split = mats[0:XD, 0:XD]
    merge = mats[0:XD, XD : 2 * XD]
    perm = mats[XD:, :]
    turn, sort = small[0], small[1]
    for q, half in enumerate(window(win, near, far)[:2]):
        tmp[...] = half
        tmp[0:64] += far[:, q * XD : (q + 1) * XD].astype(F32)
        t = tmp[0:OWN] + dot(turn, mate[q * OWN : (q + 1) * OWN, :])
        t = dot(dot(sort, t.astype(BF)).astype(BF), split)
        for s in range(2):
            for n in range(ROWS):
                bp[(q * 2 + s) * 8 : (q * 2 + s + 1) * 8, n * XC : (n + 1) * XC] = t[
                    n * 8 : (n + 1) * 8, s * XC : (s + 1) * XC
                ]
    bpb = bp[...].astype(BF)
    lane = iota((C2, XC), 1)
    for a in range(4):
        pb = lax.dot_general(wb[a], bpb, (((0,), (0,)), ((), ())), preferred_element_type=F32)
        inside = True
        if a == 0:
            inside = slab > 0
        if a == 3:
            inside = slab < 63
        for n in range(ROWS):
            lanes = slice(n * XC, (n + 1) * XC)
            if a in (1, 2):
                if n == 0:
                    v = fh[a - 1, :, :XC]
                elif n == 9:
                    v = fh[a - 1, :, XC:]
                else:
                    v = fs[a - 1, :, (n - 1) * XC : n * XC]
            else:
                half = slice((n % 2) * XC, (n % 2 + 1) * XC)
                r0 = (n // 2) * C2
                v1 = near[256 + r0 : 256 + r0 + C2, half].astype(F32)
                v2 = mate[2 * OWN + r0 : 2 * OWN + r0 + C2, half].astype(F32)
                v = jnp.where(core == (0 if a == 0 else 1), v1, v2)
            v = v + pb[:, lanes]
            v = 0.5 * v * (1.0 + jnp.tanh(0.79788456 * (v + 0.044715 * (v * v * v))))
            ok = inside
            if n == 0:
                ok = (part > 0) & ok
            if n == 9:
                ok = (part < 3) & ok
            if ok is not True:
                v = jnp.where(ok, v, 0.0)
            shifts = (
                jnp.where(lane == 0, 0.0, pltpu.roll(v, 1, 1)).astype(BF),
                v.astype(BF),
                jnp.where(lane == XC - 1, 0.0, pltpu.roll(v, XC - 1, 1)).astype(BF),
            )
            for dy in range(3):
                m = n - dy
                if 0 <= m < 8:
                    for dx in range(3):
                        r0 = a * 576 + dy * 192 + dx * C2
                        x[r0 : r0 + C2, m * XC : (m + 1) * XC] = shifts[dx]
    for f in range(ZD):
        start = (f + 1) // 2 * 576
        d = dot(wdec[f % 2], x[start : start + 1152, :])
        for py in range(2):
            for px in range(2):
                r0 = (py * 2 + px) * C1
                lanes = slice(px * XC, (px + 1) * XC)
                for m in range(8):
                    y = (2 * m + py) * C1
                    old = planes[f, y : y + C1, lanes].astype(F32)
                    ns[y : y + C1, lanes] = (old + d[r0 : r0 + C1, m * XC : (m + 1) * XC]).astype(BF)
        new = dot(dot(perm, ns[...]).astype(BF), merge).astype(BF)
        stage[f] = new.reshape(C1, YD, XD)
        pltpu.make_async_copy(stage.at[f], out.at[:, f], sems.at[f]).start()
    for f in range(ZD):
        pltpu.make_async_copy(stage.at[f], out.at[:, f], sems.at[f]).wait()


V = pltpu.VMEM
VM = pl.BlockSpec(memory_space=pltpu.VMEM)
ANY = pl.BlockSpec(memory_space=pl.ANY)


def shape(dims, dtype=BF):
    return jax.ShapeDtypeStruct(dims, dtype)


def call(kernel, ins, outs, scratch=(), cost=None, vlim=16 * MIB, outs_in=VM, **more):
    return pl.pallas_call(
        kernel,
        in_specs=ins,
        out_specs=[outs_in] * len(outs) if "grid" not in more else more.pop("specs"),
        out_shape=outs,
        scratch_shapes=scratch,
        compiler_params=pltpu.CompilerParams(vmem_limit_bytes=vlim),
        cost_estimate=cost,
        **more,
    )


def cost(us):
    return pl.CostEstimate(flops=int(us * 1e9), bytes_accessed=int(us * 3e6), transcendentals=0)


def shifted(block, axis, distance):
    n = lax.axis_size(axis)
    return lax.ppermute(block, axis, [(i, (i + distance) % n) for i in range(n)])


def swapped(block, distance):
    n = lax.axis_size("gz")
    pairs = {(i, i + distance) for i in range(0, n, 2) if 0 <= i + distance < n}
    if distance == -1:
        pairs |= {(0, 0), (n - 1, n - 1)}
    if distance == -3:
        pairs |= {(0, 2), (n - 3, n - 1)}
    route = sorted(pairs | {(j, i) for i, j in pairs})
    return lax.ppermute(block, "gz", route)


def per_device(
    state, residual, projector, pair_counts, pair_block, pair_tile, pair_view, enc_weight, dec_weight
):
    up, down, own = call(
        edge_kernel,
        [ANY] * 5,
        [shape((272, XD)), shape((272, XD)), shape((8, KL), I32)],
        [
            V((16, KL), F32),
            pltpu.SMEM((SPAN, 1, 64), I32),
            V((3, 8, NPD), I32),
            V((ZD, C1, YD, XD), BF),
            V((ZD * 128, XD), BF),
            pltpu.SemaphoreType.DMA((8,)),
        ],
        cost=cost(1.0),
        vlim=56 * MIB,
        name="edge",
    )(jnp.transpose(pair_counts, (2, 0, 1)), pair_block, pair_tile, pair_view, state)
    left = shifted(up, "gy", 1)
    right = shifted(down, "gy", -1)
    rays = jnp.transpose(residual, (1, 0, 2))
    high, low = call(
        project_kernel,
        [
            pl.BlockSpec((4, NB, DC), lambda v: (0, 0, 0)),
            pl.BlockSpec((1, DC, TILE), lambda v: (v, 0, 0)),
        ],
        [shape((4, VIEWS * NB, TILE)), shape((4, VIEWS * NB, TILE))],
        cost=cost(2.0),
        grid=(VIEWS,),
        specs=[pl.BlockSpec((4, NB, TILE), lambda v: (0, v, 0))] * 2,
        name="project",
    )(rays, projector)
    fs, planes, we, wb = call(
        encode_kernel,
        [VM] * 2,
        [
            shape((2, C2, 8 * XC), F32),
            shape((ZD, C1 * YD, XD)),
            shape((8 * C1, C2)),
            shape((4, 32, C2)),
        ],
        [V((8 * C1, 8 * XC), BF)],
        cost=cost(2.0),
        name="encode",
    )(state, jnp.transpose(enc_weight, (0, 1, 4, 2, 3)))
    win, near, far, mate, fh = call(
        place_kernel,
        [VM] * 6,
        [
            shape((CHIP, TILE), F32),
            shape((CHIP, TILE), F32),
            shape((64, TILE), F32),
            shape((112, TILE)),
            shape((2, C2, XD), F32),
        ],
        [V((8, 3 * KL), F32), V((8 * C1, 4 * XC), BF)],
        cost=cost(2.5),
        name="place",
    )(own, left, right, high, low, we)
    got = swapped(mate, 1)
    pay, pay_far = call(
        out_kernel,
        [VM] * 5,
        [shape((576, XD)), shape((64, TILE))],
        [V((128, TILE), F32)],
        cost=cost(0.4),
        name="outward",
    )(near, far, got, fs, fh)
    got_near = swapped(pay, -1)
    got_far = swapped(pay_far, -3)
    wdec, mats, small = call(
        prepare_kernel,
        [VM],
        [shape((2, 128, 1152)), shape((XD + C1 * YD, 2 * XD)), shape((2, OWN, OWN))],
        cost=cost(3.0),
        name="prepare",
    )(dec_weight)
    pay_mate = call(
        mate_kernel,
        [VM] * 5 + [ANY],
        [shape((2 * OWN + 5 * C2, XD))],
        [V((CHIP, XD), F32)],
        cost=cost(0.4),
        name="inward",
    )(win, got_near, got_far, fs, fh, small)[0]
    got_mate = swapped(pay_mate, 1)
    return call(
        decode_kernel,
        [VM] * 11,
        [shape((C1, ZD, YD, XD))],
        [
            V((32, NL), F32),
            V((2304, 8 * XC), BF),
            V((C1 * YD, XD), BF),
            V((CHIP, XD), F32),
            V((ZD, C1, YD, XD), BF),
            pltpu.SemaphoreType.DMA((ZD,)),
        ],
        outs_in=ANY,
        cost=cost(6.0),
        vlim=24 * MIB,
        name="decode",
    )(win, got_near, got_far, got_mate, fs, fh, planes, wdec, wb, mats, small)[0]


def solution(mesh):
    in_specs = (
        P(None, "gz", "gy", None),
        P("gz", None, None),
        P(),
        P("gy", None, None),
        P("gy", None, None),
        P("gy", None, None),
        P("gy", None, None),
        P(),
        P(),
    )
    out_specs = P(None, "gz", "gy", None)
    return jax.shard_map(
        per_device, mesh=mesh, in_specs=in_specs, out_specs=out_specs, check_vma=False
    )
```

```python
import functools

import jax
import jax.numpy as jnp
from jax import lax
from jax.experimental import pallas as pl
from jax.experimental.pallas import tpu as pltpu
from jax.sharding import PartitionSpec as P

C1, C2 = 32, 64
ZD, YD, XD = 4, 16, 256
XC = XD // 2
SPAN = 7
NPD = 224
VIEWS = 4
NB = 64
DC = 768
TILE = 512
KL = 256
ROWS = 10
NL = ROWS * XC
CHIP = 12 * ROWS
OWN = 8 * ROWS
FAR = 6 * ROWS
MATE = 10 * ROWS
LIST = 256
BF, F32, I32 = jnp.bfloat16, jnp.float32, jnp.int32
MIB = 1024 * 1024


def dot(a, b):
    return jnp.dot(a, b, preferred_element_type=F32)


def iota(shape, dim):
    return lax.broadcasted_iota(I32, shape, dim)


def split_columns():
    row, col = iota((XD, XD), 0), iota((XD, XD), 1)
    return (row == 2 * (col % XC) + col // XC).astype(BF)


def merge_columns():
    row, col = iota((XD, XD), 0), iota((XD, XD), 1)
    return (col == 2 * (row % XC) + row // XC).astype(BF)


def edge_kernel(counts, block, tile, view, state, up, down, own, lists, cs, pairs, planes, some, sems):
    slab = lax.axis_index("gz")
    at = pl.multiple_of((slab // 8) * 8, 8)
    copies = [pltpu.make_async_copy(counts, cs, sems.at[0])]
    for i, ref in enumerate((block, tile, view)):
        copies.append(pltpu.make_async_copy(ref.at[0, pl.ds(at, 8)], pairs.at[i], sems.at[1 + i]))
    for z in range(ZD):
        copies.append(pltpu.make_async_copy(state.at[:, z], planes.at[z], sems.at[4 + z]))
    for copy in copies:
        copy.start()
    split = split_columns()
    row, col = iota((4 * C1, C1 * YD), 0), iota((4 * C1, C1 * YD), 1)
    y = row // C1
    y = jnp.where(y < 2, y, y + YD - 4)
    pick = (col == (row % C1) * YD + y).astype(BF)
    lists[...] = jnp.full((16, KL), -1.0, F32)
    own[...] = jnp.full((8, KL), -1, I32)
    for copy in copies[:4]:
        copy.wait()
    slot = iota((1, NPD), 1)
    group = jnp.zeros((1, NPD), I32)
    end = 0
    for o in range(SPAN):
        end = end + cs[o, 0, slab]
        group = group + (slot >= end).astype(I32)
    valid = group < SPAN
    rest = pl.ds(slab % 8, 1)
    b, t, v = pairs[0, rest, :], pairs[1, rest, :], pairs[2, rest, :]
    key = v * NB + b
    own[0:1, :NPD] = key
    own[1:2, :NPD] = jnp.where(valid, group * 16 + t + 1, -1)
    lists[0:1, :NPD] = key.astype(F32)
    lists[1:2, :NPD] = jnp.where(valid & (t == 7), group, -1).astype(F32)
    up[LIST:, :] = lists[...].astype(BF)
    lists[1:2, :NPD] = jnp.where(valid & (t == 0), group, -1).astype(F32)
    down[LIST:, :] = lists[...].astype(BF)
    for z in range(ZD):
        copies[4 + z].wait()
        some[z * 128 : (z + 1) * 128, :] = dot(pick, planes[z].reshape(C1 * YD, XD)).astype(BF)
    rows = dot(some[...], split).astype(BF)
    for z in range(ZD):
        down[z * 64 : z * 64 + 64, :] = rows[z * 128 : z * 128 + 64]
        up[z * 64 : z * 64 + 64, :] = rows[z * 128 + 64 : z * 128 + 128]


def project_kernel(res, proj, flat, high, low):
    y = dot(res[...].reshape(4 * NB, DC), proj[0])
    hi = y.astype(BF)
    lo = (y - hi.astype(F32)).astype(BF)
    for r in range(4):
        high[r] = hi[r * NB : (r + 1) * NB]
        low[r] = lo[r * NB : (r + 1) * NB]


def flat_kernel(state, flat):
    split = split_columns()
    for z in range(ZD):
        flat[z] = dot(state[:, z].reshape(C1 * YD, XD), split).astype(BF)


def place_kernel(own, left, right, high, low, small, win, near, far, mate, keys):
    slab, part = lax.axis_index("gz"), lax.axis_index("gy")
    core = slab % 2
    keys[0:1, 0:KL] = own[0:1, :].astype(F32)
    keys[1:2, 0:KL] = own[1:2, :].astype(F32)
    lk = left[LIST:, :].astype(F32)
    rk = right[LIST:, :].astype(F32)
    keys[0:1, KL : 2 * KL] = lk[0:1]
    keys[0:1, 2 * KL :] = rk[0:1]
    lg, rg = lk[1:2], rk[1:2]
    keys[1:2, KL : 2 * KL] = jnp.where((lg >= 0) & (part > 0), lg * 16, -1.0)
    keys[1:2, 2 * KL :] = jnp.where((rg >= 0) & (part < 3), rg * 16 + 9, -1.0)
    key = keys[0:1, :].astype(I32)
    skey = keys[1:2, :].astype(I32)
    total = 416
    row = iota((total, 1), 0)

    def pieces(values):
        w, n, m, f = values
        return jnp.where(row < 120, w, jnp.where(row < 240, n, jnp.where(row < 352, m, f)))

    k = row - pieces((0, 120, 240, 352))
    t = k // ROWS
    n = k % ROWS
    even = core == 0
    first = jnp.where(even, pieces((-2, 1, 6, -7)), pieces((5, 2, -3, 10)))
    step = jnp.where(even, pieces((1, -1, 1, -1)), pieces((-1, 1, -1, 1)))
    s = first + step * t + 12
    rkey = jnp.where(t < pieces((12, 12, 10, 6)), (s // 4) * 16 + n, -2)
    r = s % 4
    a = (rkey == skey).astype(BF)
    bk = (iota((VIEWS * NB, 1), 0) == key).astype(BF)
    count = lax.dot_general(a, bk, (((1,), (1,)), ((), ())), preferred_element_type=F32)
    each = jnp.concatenate([jnp.where(r == q, count, 0.0).astype(BF) for q in range(4)], axis=1)
    acc = dot(each, high[...].reshape(4 * VIEWS * NB, TILE)) + dot(each, low[...].reshape(4 * VIEWS * NB, TILE))
    win[...] = acc[:120]
    near[...] = acc[120:240]
    mate[...] = acc[240:352].astype(BF)
    far[...] = acc[352:]


def encode_kernel(flat, left, right, enc, fs, out, keep, wb, we, x, wide):
    rows = iota((32, C2), 0)
    bias = [jnp.zeros((32, C2), F32) for _ in range(4)]
    for p in range(2):
        for q in range(2):
            e = enc[p, q].astype(F32)
            for s in range(2):
                k = p * 4 + q * 2 + s
                es = e[:, s, :]
                we[k * C1 : (k + 1) * C1, :] = es[:C1].astype(BF)
                for a in range(4):
                    bias[a] = bias[a] + jnp.where(rows == (q * 2 + s) * 8 + 2 * a + p, es[C1 : C1 + 1], 0.0)
    for a in range(4):
        wb[a] = bias[a].astype(BF)
    for z in range(ZD):
        for s in range(2):
            wide[z * 2 + s] = flat[z, :, s * XC : (s + 1) * XC].astype(F32)
    for a in range(2):
        for p in range(2):
            z = 2 * a + p
            for q in range(2):
                for s in range(2):
                    k = (p * 4 + q * 2 + s) * C1
                    lanes = slice(s * XC, (s + 1) * XC)
                    h = z * 64 + q * C1
                    x[k : k + C1, 0:XC] = left[h : h + C1, lanes]
                    x[k : k + C1, 9 * XC : 10 * XC] = right[h : h + C1, lanes]
                    for b in range(8):
                        y = wide[z * 2 + s, pl.ds(2 * b + q, C1, stride=YD), :]
                        x[k : k + C1, (b + 1) * XC : (b + 2) * XC] = y.astype(BF)
        f = lax.dot_general(we[...], x[...], (((0,), (0,)), ((), ())), preferred_element_type=F32)
        fs[a] = f

        def put(ref, f=f):
            for t in range(5):
                ref[t * C2 : (t + 1) * C2, :] = f[:, t * XD : (t + 1) * XD].astype(BF)

        mine = lax.axis_index("gz") % 2 == a
        pl.when(mine)(functools.partial(put, out))
        pl.when(jnp.logical_not(mine))(functools.partial(put, keep))


def prepare_kernel(dec, wdec, mats, small):
    mats[0:XD, 0:XD] = split_columns()
    mats[0:XD, XD : 2 * XD] = merge_columns()
    core = lax.axis_index("gz") % 2
    row, col = iota((OWN, OWN), 0), iota((OWN, OWN), 1)
    small[0] = ((col % ROWS == row % ROWS) & (col // ROWS == 7 - row // ROWS)).astype(BF)
    z = row % 8
    z = jnp.where(core == 0, z, 7 - z)
    small[1] = ((col % ROWS == row // 8) & (col // ROWS == z)).astype(BF)
    wdec[...] = jnp.zeros_like(wdec)
    taps = (((0, 3), (1, 1)), ((1, 2), (2, 0)))
    for pz in range(2):
        for sel in range(2):
            kz = taps[pz][sel][1]
            for py in range(2):
                for dy, ky in taps[py]:
                    for px in range(2):
                        for dx, kx in taps[px]:
                            r0 = (py * 2 + px) * C1
                            c0 = (sel * 9 + dy * 3 + dx) * C2
                            wdec[pz, r0 : r0 + C1, c0 : c0 + C2] = dec[kz, ky, kx]


def out_kernel(near, far, got, pre, pay, pay_far, tmp):
    tmp[0:CHIP] = near[...]
    tmp[CHIP:128] = jnp.zeros((8, TILE), F32)
    tmp[0:MATE] += got[...].astype(F32)[:MATE]
    total = tmp[...].astype(BF)
    pay[0:128, :] = total[:, :XD]
    pay[128:256, :] = total[:, XD:]
    pay[256:, :] = pre[...]
    tmp[0:64] = far[...]
    tmp[0 : 2 * ROWS] += got[...].astype(F32)[8 * ROWS : MATE]
    pay_far[...] = tmp[0:64].astype(BF)


def add_near(tmp, win, near):
    tmp[:, :XD] = win[:, :XD] + near[0:128, :].astype(F32)[:CHIP]
    tmp[:, XD:] = win[:, XD:] + near[128:256, :].astype(F32)[:CHIP]


def mate_kernel(win, near, far, pre, pay, tmp):
    add_near(tmp, win, near)
    tmp[0:64] += far[...].astype(F32)
    total = tmp[CHIP - OWN :, :].astype(BF)
    pay[0:OWN, :] = total[:, :XD]
    pay[OWN : 2 * OWN, :] = total[:, XD:]
    pay[2 * OWN :, :] = pre[...]


def decode_kernel(win, near, far, mate, fs, flat, wdec, wb, mats, small, out, bp, x, ns, tmp, stage, sems):
    slab, part = lax.axis_index("gz"), lax.axis_index("gy")
    core = slab % 2
    split = mats[0:XD, 0:XD]
    merge = mats[0:XD, XD : 2 * XD]
    turn, sort = small[0], small[1]
    add_near(tmp, win, near)
    tmp[0:64] += far[...].astype(F32)
    for q in range(2):
        t = tmp[0:OWN, q * XD : (q + 1) * XD] + dot(turn, mate[q * OWN : (q + 1) * OWN, :])
        t = dot(dot(sort, t.astype(BF)).astype(BF), split)
        for s in range(2):
            for n in range(ROWS):
                bp[(q * 2 + s) * 8 : (q * 2 + s + 1) * 8, n * XC : (n + 1) * XC] = t[
                    n * 8 : (n + 1) * 8, s * XC : (s + 1) * XC
                ]
    bpb = bp[...].astype(BF)
    lane = iota((C2, XC), 1)
    for a in range(4):
        pb = lax.dot_general(wb[a], bpb, (((0,), (0,)), ((), ())), preferred_element_type=F32)
        inside = True
        if a == 0:
            inside = slab > 0
        if a == 3:
            inside = slab < 63
        for n in range(ROWS):
            lanes = slice(n * XC, (n + 1) * XC)
            if a in (1, 2):
                v = fs[a - 1, :, lanes]
            else:
                half = slice((n % 2) * XC, (n % 2 + 1) * XC)
                r0 = (n // 2) * C2
                v1 = near[256 + r0 : 256 + r0 + C2, half].astype(F32)
                v2 = mate[2 * OWN + r0 : 2 * OWN + r0 + C2, half].astype(F32)
                v = jnp.where(core == (0 if a == 0 else 1), v1, v2)
            v = v + pb[:, lanes]
            v = 0.5 * v * (1.0 + jnp.tanh(0.79788456 * (v + 0.044715 * (v * v * v))))
            ok = inside
            if n == 0:
                ok = (part > 0) & ok
            if n == 9:
                ok = (part < 3) & ok
            if ok is not True:
                v = jnp.where(ok, v, 0.0)
            shifts = (
                jnp.where(lane == 0, 0.0, pltpu.roll(v, 1, 1)).astype(BF),
                v.astype(BF),
                jnp.where(lane == XC - 1, 0.0, pltpu.roll(v, XC - 1, 1)).astype(BF),
            )
            for dy in range(3):
                m = n - dy
                if 0 <= m < 8:
                    for dx in range(3):
                        r0 = a * 576 + dy * 192 + dx * C2
                        x[r0 : r0 + C2, m * XC : (m + 1) * XC] = shifts[dx]
    for f in range(ZD):
        start = (f + 1) // 2 * 576
        d = dot(wdec[f % 2], x[start : start + 1152, :])
        for py in range(2):
            for px in range(2):
                r0 = (py * 2 + px) * C1
                for m in range(8):
                    ns[px, pl.ds(2 * m + py, C1, stride=YD), :] = d[r0 : r0 + C1, m * XC : (m + 1) * XC]
        both = jnp.concatenate([ns[0], ns[1]], axis=1)
        new = dot((flat[f].astype(F32) + both).astype(BF), merge).astype(BF)
        stage[f] = new.reshape(C1, YD, XD)
        pltpu.make_async_copy(stage.at[f], out.at[:, f], sems.at[f]).start()
    for f in range(ZD):
        pltpu.make_async_copy(stage.at[f], out.at[:, f], sems.at[f]).wait()


V = pltpu.VMEM
VM = pl.BlockSpec(memory_space=pltpu.VMEM)
ANY = pl.BlockSpec(memory_space=pl.ANY)


def shape(dims, dtype=BF):
    return jax.ShapeDtypeStruct(dims, dtype)


def call(kernel, ins, outs, scratch=(), cost=None, vlim=16 * MIB, outs_in=VM, **more):
    return pl.pallas_call(
        kernel,
        in_specs=ins,
        out_specs=[outs_in] * len(outs) if "grid" not in more else more.pop("specs"),
        out_shape=outs,
        scratch_shapes=scratch,
        compiler_params=pltpu.CompilerParams(vmem_limit_bytes=vlim),
        cost_estimate=cost,
        **more,
    )


def cost(us):
    return pl.CostEstimate(flops=int(us * 1e9), bytes_accessed=int(us * 3e6), transcendentals=0)


def shifted(block, axis, distance):
    n = lax.axis_size(axis)
    return lax.ppermute(block, axis, [(i, (i + distance) % n) for i in range(n)])


def swapped(block, distance):
    n, m = lax.axis_size("gz"), lax.axis_size("gy")
    pairs = {(i, i + distance) for i in range(0, n, 2) if 0 <= i + distance < n}
    if distance == -3:
        pairs |= {(0, 2), (n - 3, n - 1)}
    pairs = {(i * m + k, j * m + k) for i, j in pairs for k in range(m)}
    if distance == -1:
        pairs |= {(i * m + k, i * m + k + 1) for i in (0, n - 1) for k in range(0, m, 2)}
    return lax.ppermute(block, ("gz", "gy"), sorted(pairs | {(j, i) for i, j in pairs}))


def per_device(
    state, residual, projector, pair_counts, pair_block, pair_tile, pair_view, enc_weight, dec_weight
):
    up, down, own = call(
        edge_kernel,
        [ANY] * 5,
        [shape((272, XD)), shape((272, XD)), shape((8, KL), I32)],
        [
            V((16, KL), F32),
            pltpu.SMEM((SPAN, 1, 64), I32),
            V((3, 8, NPD), I32),
            V((ZD, C1, YD, XD), BF),
            V((ZD * 128, XD), BF),
            pltpu.SemaphoreType.DMA((8,)),
        ],
        cost=cost(2.9),
        vlim=56 * MIB,
        name="edge",
    )(jnp.transpose(pair_counts, (2, 0, 1)), pair_block, pair_tile, pair_view, state)
    left = shifted(up, "gy", 1)
    right = shifted(down, "gy", -1)
    flat = call(flat_kernel, [VM], [shape((ZD, C1 * YD, XD))], cost=cost(0.4), name="flat")(state)[0]
    rays = jnp.transpose(residual, (1, 0, 2))
    high, low = call(
        project_kernel,
        [
            pl.BlockSpec((4, NB, DC), lambda v: (0, 0, 0)),
            pl.BlockSpec((1, DC, TILE), lambda v: (v, 0, 0)),
            ANY,
        ],
        [shape((4, VIEWS * NB, TILE)), shape((4, VIEWS * NB, TILE))],
        cost=cost(1.7),
        grid=(VIEWS,),
        specs=[pl.BlockSpec((4, NB, TILE), lambda v: (0, v, 0))] * 2,
        name="project",
    )(rays, projector, flat)
    wdec, mats, small = call(
        prepare_kernel,
        [VM],
        [shape((2, 128, 1152)), shape((XD, 2 * XD)), shape((2, OWN, OWN))],
        cost=cost(0.3),
        name="prepare",
    )(dec_weight)
    win, near, far, mate = call(
        place_kernel,
        [VM] * 5 + [ANY],
        [
            shape((CHIP, TILE), F32),
            shape((CHIP, TILE), F32),
            shape((64, TILE), F32),
            shape((112, TILE)),
        ],
        [V((8, 3 * KL), F32)],
        cost=cost(1.5),
        name="place",
    )(own, left, right, high, low, small)
    got = swapped(mate, 1)
    fs, pre_out, pre_mate, wb = call(
        encode_kernel,
        [VM] * 4,
        [shape((2, C2, NL), F32), shape((5 * C2, XD)), shape((5 * C2, XD)), shape((4, 32, C2))],
        [V((8 * C1, C2), BF), V((8 * C1, NL), BF), V((2 * ZD, C1 * YD, XC), F32)],
        cost=cost(1.5),
        name="encode",
    )(flat, left, right, jnp.transpose(enc_weight, (0, 1, 4, 2, 3)))
    pay, pay_far = call(
        out_kernel,
        [VM] * 4,
        [shape((576, XD)), shape((64, TILE))],
        [V((128, TILE), F32)],
        cost=cost(0.1),
        name="outward",
    )(near, far, got, pre_out)
    got_near = swapped(pay, -1)
    got_far = swapped(pay_far, -3)
    pay_mate = call(
        mate_kernel,
        [VM] * 4,
        [shape((2 * OWN + 5 * C2, XD))],
        [V((CHIP, TILE), F32)],
        cost=cost(0.1),
        name="inward",
    )(win, got_near, got_far, pre_mate)[0]
    got_mate = swapped(pay_mate, 1)
    return call(
        decode_kernel,
        [VM] * 10,
        [shape((C1, ZD, YD, XD))],
        [
            V((32, NL), F32),
            V((2304, 8 * XC), BF),
            V((2, C1 * YD, XC), F32),
            V((CHIP, TILE), F32),
            V((ZD, C1, YD, XD), BF),
            pltpu.SemaphoreType.DMA((ZD,)),
        ],
        outs_in=ANY,
        cost=cost(5.0),
        vlim=24 * MIB,
        name="decode",
    )(win, got_near, got_far, got_mate, fs, flat, wdec, wb, mats, small)[0]


def solution(mesh):
    in_specs = (
        P(None, "gz", "gy", None),
        P("gz", None, None),
        P(),
        P("gy", None, None),
        P("gy", None, None),
        P("gy", None, None),
        P("gy", None, None),
        P(),
        P(),
    )
    out_specs = P(None, "gz", "gy", None)
    return jax.shard_map(
        per_device, mesh=mesh, in_specs=in_specs, out_specs=out_specs, check_vma=False
    )
```

```python
import functools

import jax
import jax.numpy as jnp
from jax import lax
from jax.experimental import pallas as pl
from jax.experimental.pallas import tpu as pltpu
from jax.sharding import PartitionSpec as P

C1, C2 = 32, 64
ZD, YD, XD = 4, 16, 256
XC = XD // 2
SPAN = 7
NPD = 224
VIEWS = 4
NB = 64
DC = 768
TILE = 512
KL = 256
ROWS = 10
NL = ROWS * XC
CHIP = 12 * ROWS
OWN = 8 * ROWS
FAR = 6 * ROWS
MATE = 10 * ROWS
LIST = 256
BF, F32, I32 = jnp.bfloat16, jnp.float32, jnp.int32
MIB = 1024 * 1024


def dot(a, b):
    return jnp.dot(a, b, preferred_element_type=F32)


def iota(shape, dim):
    return lax.broadcasted_iota(I32, shape, dim)


def split_columns():
    row, col = iota((XD, XD), 0), iota((XD, XD), 1)
    return (row == 2 * (col % XC) + col // XC).astype(BF)


def merge_columns():
    row, col = iota((XD, XD), 0), iota((XD, XD), 1)
    return (col == 2 * (row % XC) + row // XC).astype(BF)


def edge_kernel(counts, block, tile, view, state, up, down, own, lists, cs, pairs, planes, some, sems):
    slab = lax.axis_index("gz")
    at = pl.multiple_of((slab // 8) * 8, 8)
    copies = [pltpu.make_async_copy(counts, cs, sems.at[0])]
    for i, ref in enumerate((block, tile, view)):
        copies.append(pltpu.make_async_copy(ref.at[0, pl.ds(at, 8)], pairs.at[i], sems.at[1 + i]))
    for z in range(ZD):
        copies.append(pltpu.make_async_copy(state.at[:, z], planes.at[z], sems.at[4 + z]))
    for copy in copies:
        copy.start()
    split = split_columns()
    row, col = iota((4 * C1, C1 * YD), 0), iota((4 * C1, C1 * YD), 1)
    y = row // C1
    y = jnp.where(y < 2, y, y + YD - 4)
    pick = (col == (row % C1) * YD + y).astype(BF)
    lists[...] = jnp.full((16, KL), -1.0, F32)
    own[...] = jnp.full((8, KL), -1, I32)
    for copy in copies[:4]:
        copy.wait()
    slot = iota((1, NPD), 1)
    group = jnp.zeros((1, NPD), I32)
    end = 0
    for o in range(SPAN):
        end = end + cs[o, 0, slab]
        group = group + (slot >= end).astype(I32)
    valid = group < SPAN
    rest = pl.ds(slab % 8, 1)
    b, t, v = pairs[0, rest, :], pairs[1, rest, :], pairs[2, rest, :]
    key = v * NB + b
    own[0:1, :NPD] = key
    own[1:2, :NPD] = jnp.where(valid, group * 16 + t + 1, -1)
    lists[0:1, :NPD] = key.astype(F32)
    lists[1:2, :NPD] = jnp.where(valid & (t == 7), group, -1).astype(F32)
    up[LIST:, :] = lists[...].astype(BF)
    lists[1:2, :NPD] = jnp.where(valid & (t == 0), group, -1).astype(F32)
    down[LIST:, :] = lists[...].astype(BF)
    for z in range(ZD):
        copies[4 + z].wait()
        some[z * 128 : (z + 1) * 128, :] = dot(pick, planes[z].reshape(C1 * YD, XD)).astype(BF)
    rows = dot(some[...], split).astype(BF)
    for z in range(ZD):
        down[z * 64 : z * 64 + 64, :] = rows[z * 128 : z * 128 + 64]
        up[z * 64 : z * 64 + 64, :] = rows[z * 128 + 64 : z * 128 + 128]


def project_kernel(res, proj, flat, high, low):
    y = dot(res[...].reshape(4 * NB, DC), proj[0])
    hi = y.astype(BF)
    lo = (y - hi.astype(F32)).astype(BF)
    for r in range(4):
        high[r] = hi[r * NB : (r + 1) * NB]
        low[r] = lo[r * NB : (r + 1) * NB]


def flat_kernel(state, flat):
    split = split_columns()
    for z in range(ZD):
        flat[z] = dot(state[:, z].reshape(C1 * YD, XD), split).astype(BF)


def place_kernel(own, left, right, high, low, fs, win, near, far, mate, out, keys):
    slab, part = lax.axis_index("gz"), lax.axis_index("gy")
    core = slab % 2
    keys[0:1, 0:KL] = own[0:1, :].astype(F32)
    keys[1:2, 0:KL] = own[1:2, :].astype(F32)
    lk = left[LIST:, :].astype(F32)
    rk = right[LIST:, :].astype(F32)
    keys[0:1, KL : 2 * KL] = lk[0:1]
    keys[0:1, 2 * KL :] = rk[0:1]
    lg, rg = lk[1:2], rk[1:2]
    keys[1:2, KL : 2 * KL] = jnp.where((lg >= 0) & (part > 0), lg * 16, -1.0)
    keys[1:2, 2 * KL :] = jnp.where((rg >= 0) & (part < 3), rg * 16 + 9, -1.0)
    key = keys[0:1, :].astype(I32)
    skey = keys[1:2, :].astype(I32)
    total = 416
    row = iota((total, 1), 0)

    def pieces(values):
        w, n, m, f = values
        return jnp.where(row < 120, w, jnp.where(row < 240, n, jnp.where(row < 352, m, f)))

    k = row - pieces((0, 120, 240, 352))
    t = k // ROWS
    n = k % ROWS
    even = core == 0
    first = jnp.where(even, pieces((-2, 1, 6, -7)), pieces((5, 2, -3, 10)))
    step = jnp.where(even, pieces((1, -1, 1, -1)), pieces((-1, 1, -1, 1)))
    s = first + step * t + 12
    rkey = jnp.where(t < pieces((12, 12, 10, 6)), (s // 4) * 16 + n, -2)
    r = s % 4
    a = (rkey == skey).astype(BF)
    bk = (iota((VIEWS * NB, 1), 0) == key).astype(BF)
    count = lax.dot_general(a, bk, (((1,), (1,)), ((), ())), preferred_element_type=F32)
    each = jnp.concatenate([jnp.where(r == q, count, 0.0).astype(BF) for q in range(4)], axis=1)
    acc = dot(each, high[...].reshape(4 * VIEWS * NB, TILE)) + dot(each, low[...].reshape(4 * VIEWS * NB, TILE))
    win[...] = acc[:120]
    near[...] = acc[120:240]
    mate[...] = acc[240:352].astype(BF)
    far[...] = acc[352:]
    for t in range(4):
        out[t * C2 : (t + 1) * C2, :] = fs[core, :, t * XD : (t + 1) * XD].astype(BF)


def encode_kernel(flat, enc, fs, wb, we, x, wide):
    rows = iota((32, C2), 0)
    bias = [jnp.zeros((32, C2), F32) for _ in range(4)]
    for p in range(2):
        for q in range(2):
            e = enc[p, q].astype(F32)
            for s in range(2):
                k = p * 4 + q * 2 + s
                es = e[:, s, :]
                we[k * C1 : (k + 1) * C1, :] = es[:C1].astype(BF)
                for a in range(4):
                    bias[a] = bias[a] + jnp.where(rows == (q * 2 + s) * 8 + 2 * a + p, es[C1 : C1 + 1], 0.0)
    for a in range(4):
        wb[a] = bias[a].astype(BF)
    for z in range(ZD):
        for s in range(2):
            wide[z * 2 + s] = flat[z, :, s * XC : (s + 1) * XC].astype(F32)
    for a in range(2):
        for p in range(2):
            z = 2 * a + p
            for q in range(2):
                for s in range(2):
                    k = (p * 4 + q * 2 + s) * C1
                    for b in range(8):
                        y = wide[z * 2 + s, pl.ds(2 * b + q, C1, stride=YD), :]
                        x[k : k + C1, b * XC : (b + 1) * XC] = y.astype(BF)
        f = lax.dot_general(we[...], x[...], (((0,), (0,)), ((), ())), preferred_element_type=F32)
        fs[a] = f


def halo_kernel(left, right, we, fs, fh, edge, keep, x):
    for a in range(2):
        for p in range(2):
            for q in range(2):
                for s in range(2):
                    k = (p * 4 + q * 2 + s) * C1
                    lanes = slice(s * XC, (s + 1) * XC)
                    h = (2 * a + p) * 64 + q * C1
                    x[k : k + C1, 2 * a * XC : (2 * a + 1) * XC] = left[h : h + C1, lanes]
                    x[k : k + C1, (2 * a + 1) * XC : (2 * a + 2) * XC] = right[h : h + C1, lanes]
    f = lax.dot_general(we[...], x[...], (((0,), (0,)), ((), ())), preferred_element_type=F32)
    for a in range(2):
        fh[a] = f[:, a * XD : (a + 1) * XD]
    core = lax.axis_index("gz") % 2
    edge[...] = fh[core].astype(BF)
    for t in range(4):
        keep[t * C2 : (t + 1) * C2, :] = fs[1 - core, :, t * XD : (t + 1) * XD].astype(BF)
    keep[4 * C2 :, :] = fh[1 - core].astype(BF)


def prepare_kernel(dec, beyond, wdec, mats, small):
    mats[0:XD, 0:XD] = split_columns()
    mats[0:XD, XD : 2 * XD] = merge_columns()
    core = lax.axis_index("gz") % 2
    row, col = iota((OWN, OWN), 0), iota((OWN, OWN), 1)
    small[0] = ((col % ROWS == row % ROWS) & (col // ROWS == 7 - row // ROWS)).astype(BF)
    z = row % 8
    z = jnp.where(core == 0, z, 7 - z)
    small[1] = ((col % ROWS == row // 8) & (col // ROWS == z)).astype(BF)
    wdec[...] = jnp.zeros_like(wdec)
    taps = (((0, 3), (1, 1)), ((1, 2), (2, 0)))
    for pz in range(2):
        for sel in range(2):
            kz = taps[pz][sel][1]
            for py in range(2):
                for dy, ky in taps[py]:
                    for px in range(2):
                        for dx, kx in taps[px]:
                            r0 = (py * 2 + px) * C1
                            c0 = (sel * 9 + dy * 3 + dx) * C2
                            wdec[pz, r0 : r0 + C1, c0 : c0 + C2] = dec[kz, ky, kx]


def out_kernel(near, far, got, edge, pay, pay_far, tmp):
    tmp[0:CHIP] = near[...]
    tmp[CHIP:128] = jnp.zeros((8, TILE), F32)
    tmp[0:MATE] += got[...].astype(F32)[:MATE]
    total = tmp[...].astype(BF)
    pay[0:128, :] = total[:, :XD]
    pay[128:256, :] = total[:, XD:]
    pay[256:, :] = edge[...]
    tmp[0:64] = far[...]
    tmp[0 : 2 * ROWS] += got[...].astype(F32)[8 * ROWS : MATE]
    pay_far[...] = tmp[0:64].astype(BF)


def add_near(tmp, win, near):
    tmp[:, :XD] = win[:, :XD] + near[0:128, :].astype(F32)[:CHIP]
    tmp[:, XD:] = win[:, XD:] + near[128:256, :].astype(F32)[:CHIP]


def mate_kernel(win, near, far, pre, small, pay, tmp):
    add_near(tmp, win, near)
    tmp[0:64] += far[...].astype(F32)
    total = tmp[CHIP - OWN :, :].astype(BF)
    pay[0:OWN, :] = total[:, :XD]
    pay[OWN : 2 * OWN, :] = total[:, XD:]
    pay[2 * OWN :, :] = pre[...]


def decode_kernel(win, near, far, mate, beyond, fs, fh, flat, wdec, wb, mats, small, out, bp, x, ns, tmp, stage, sems):
    slab, part = lax.axis_index("gz"), lax.axis_index("gy")
    core = slab % 2
    split = mats[0:XD, 0:XD]
    merge = mats[0:XD, XD : 2 * XD]
    turn, sort = small[0], small[1]
    add_near(tmp, win, near)
    tmp[0:64] += far[...].astype(F32)
    for q in range(2):
        t = tmp[0:OWN, q * XD : (q + 1) * XD] + dot(turn, mate[q * OWN : (q + 1) * OWN, :])
        t = dot(dot(sort, t.astype(BF)).astype(BF), split)
        for s in range(2):
            for n in range(ROWS):
                bp[(q * 2 + s) * 8 : (q * 2 + s + 1) * 8, n * XC : (n + 1) * XC] = t[
                    n * 8 : (n + 1) * 8, s * XC : (s + 1) * XC
                ]
    bpb = bp[...].astype(BF)
    lane = iota((C2, XC), 1)
    for a in range(4):
        pb = lax.dot_general(wb[a], bpb, (((0,), (0,)), ((), ())), preferred_element_type=F32)
        inside = True
        if a == 0:
            inside = slab > 0
        if a == 3:
            inside = slab < 63
        for n in range(ROWS):
            outer = n in (0, 9)
            half = slice((n != 0) * XC, ((n != 0) + 1) * XC) if outer else slice((n - 1) % 2 * XC, ((n - 1) % 2 + 1) * XC)
            if a in (1, 2):
                v = fh[a - 1, :, half] if outer else fs[a - 1, :, (n - 1) * XC : n * XC]
            else:
                r0 = 4 * C2 if outer else (n - 1) // 2 * C2
                v1 = (near[256:, half] if outer else beyond[r0 : r0 + C2, half]).astype(F32)
                v2 = mate[2 * OWN + r0 : 2 * OWN + r0 + C2, half].astype(F32)
                v = jnp.where(core == (0 if a == 0 else 1), v1, v2)
            v = v + pb[:, n * XC : (n + 1) * XC]
            v = 0.5 * v * (1.0 + jnp.tanh(0.79788456 * (v + 0.044715 * (v * v * v))))
            ok = inside
            if n == 0:
                ok = (part > 0) & ok
            if n == 9:
                ok = (part < 3) & ok
            if ok is not True:
                v = jnp.where(ok, v, 0.0)
            shifts = (
                jnp.where(lane == 0, 0.0, pltpu.roll(v, 1, 1)).astype(BF),
                v.astype(BF),
                jnp.where(lane == XC - 1, 0.0, pltpu.roll(v, XC - 1, 1)).astype(BF),
            )
            for dy in range(3):
                m = n - dy
                if 0 <= m < 8:
                    for dx in range(3):
                        r0 = a * 576 + dy * 192 + dx * C2
                        x[r0 : r0 + C2, m * XC : (m + 1) * XC] = shifts[dx]
    for f in range(ZD):
        start = (f + 1) // 2 * 576
        d = dot(wdec[f % 2], x[start : start + 1152, :])
        for py in range(2):
            for px in range(2):
                r0 = (py * 2 + px) * C1
                for m in range(8):
                    ns[px, pl.ds(2 * m + py, C1, stride=YD), :] = d[r0 : r0 + C1, m * XC : (m + 1) * XC]
        both = jnp.concatenate([ns[0], ns[1]], axis=1)
        new = dot((flat[f].astype(F32) + both).astype(BF), merge).astype(BF)
        stage[f] = new.reshape(C1, YD, XD)
        pltpu.make_async_copy(stage.at[f], out.at[:, f], sems.at[f]).start()
    for f in range(ZD):
        pltpu.make_async_copy(stage.at[f], out.at[:, f], sems.at[f]).wait()


V = pltpu.VMEM
VM = pl.BlockSpec(memory_space=pltpu.VMEM)
ANY = pl.BlockSpec(memory_space=pl.ANY)


def shape(dims, dtype=BF):
    return jax.ShapeDtypeStruct(dims, dtype)


def call(kernel, ins, outs, scratch=(), cost=None, vlim=16 * MIB, outs_in=VM, **more):
    return pl.pallas_call(
        kernel,
        in_specs=ins,
        out_specs=[outs_in] * len(outs) if "grid" not in more else more.pop("specs"),
        out_shape=outs,
        scratch_shapes=scratch,
        compiler_params=pltpu.CompilerParams(vmem_limit_bytes=vlim),
        cost_estimate=cost,
        **more,
    )


def cost(us):
    return pl.CostEstimate(flops=int(us * 1e9), bytes_accessed=int(us * 3e6), transcendentals=0)


def shifted(block, axis, distance):
    n = lax.axis_size(axis)
    return lax.ppermute(block, axis, [(i, (i + distance) % n) for i in range(n)])


def swapped(block, distance):
    n, m = lax.axis_size("gz"), lax.axis_size("gy")
    pairs = {(i, i + distance) for i in range(0, n, 2) if 0 <= i + distance < n}
    if distance == -3:
        pairs |= {(0, 2), (n - 3, n - 1)}
    pairs = {(i * m + k, j * m + k) for i, j in pairs for k in range(m)}
    if distance == -1:
        pairs |= {(i * m + k, i * m + k + 1) for i in (0, n - 1) for k in range(0, m, 2)}
    return lax.ppermute(block, ("gz", "gy"), sorted(pairs | {(j, i) for i, j in pairs}))


def per_device(
    state, residual, projector, pair_counts, pair_block, pair_tile, pair_view, enc_weight, dec_weight
):
    up, down, own = call(
        edge_kernel,
        [ANY] * 5,
        [shape((272, XD)), shape((272, XD)), shape((8, KL), I32)],
        [
            V((16, KL), F32),
            pltpu.SMEM((SPAN, 1, 64), I32),
            V((3, 8, NPD), I32),
            V((ZD, C1, YD, XD), BF),
            V((ZD * 128, XD), BF),
            pltpu.SemaphoreType.DMA((8,)),
        ],
        cost=cost(2.9),
        vlim=56 * MIB,
        name="edge",
    )(jnp.transpose(pair_counts, (2, 0, 1)), pair_block, pair_tile, pair_view, state)
    left = shifted(up, "gy", 1)
    right = shifted(down, "gy", -1)
    flat = call(flat_kernel, [VM], [shape((ZD, C1 * YD, XD))], cost=cost(0.4), name="flat")(state)[0]
    rays = jnp.transpose(residual, (1, 0, 2))
    high, low = call(
        project_kernel,
        [
            pl.BlockSpec((4, NB, DC), lambda v: (0, 0, 0)),
            pl.BlockSpec((1, DC, TILE), lambda v: (v, 0, 0)),
            ANY,
        ],
        [shape((4, VIEWS * NB, TILE)), shape((4, VIEWS * NB, TILE))],
        cost=cost(1.7),
        grid=(VIEWS,),
        specs=[pl.BlockSpec((4, NB, TILE), lambda v: (0, v, 0))] * 2,
        name="project",
    )(rays, projector, flat)
    fs, wb, we = call(
        encode_kernel,
        [VM] * 2,
        [shape((2, C2, 8 * XC), F32), shape((4, 32, C2)), shape((8 * C1, C2))],
        [V((8 * C1, 8 * XC), BF), V((2 * ZD, C1 * YD, XC), F32)],
        cost=cost(1.3),
        name="encode",
    )(flat, jnp.transpose(enc_weight, (0, 1, 4, 2, 3)))
    win, near, far, mate, pre_out = call(
        place_kernel,
        [VM] * 6,
        [
            shape((CHIP, TILE), F32),
            shape((CHIP, TILE), F32),
            shape((64, TILE), F32),
            shape((112, TILE)),
            shape((4 * C2, XD)),
        ],
        [V((8, 3 * KL), F32)],
        cost=cost(1.5),
        name="place",
    )(own, left, right, high, low, fs)
    got = swapped(mate, 1)
    beyond = swapped(pre_out, -1)
    fh, edge, pre_mate = call(
        halo_kernel,
        [VM] * 4,
        [shape((2, C2, XD), F32), shape((C2, XD)), shape((5 * C2, XD))],
        [V((8 * C1, 4 * XC), BF)],
        cost=cost(0.5),
        name="halo",
    )(left, right, we, fs)
    pay, pay_far = call(
        out_kernel,
        [VM] * 4,
        [shape((320, XD)), shape((64, TILE))],
        [V((128, TILE), F32)],
        cost=cost(0.1),
        name="outward",
    )(near, far, got, edge)
    got_near = swapped(pay, -1)
    got_far = swapped(pay_far, -3)
    wdec, mats, small = call(
        prepare_kernel,
        [VM, ANY],
        [shape((2, 128, 1152)), shape((XD, 2 * XD)), shape((2, OWN, OWN))],
        cost=cost(4.0),
        name="prepare",
    )(dec_weight, beyond)
    pay_mate = call(
        mate_kernel,
        [VM] * 4 + [ANY],
        [shape((2 * OWN + 5 * C2, XD))],
        [V((CHIP, TILE), F32)],
        cost=cost(0.1),
        name="inward",
    )(win, got_near, got_far, pre_mate, small)[0]
    got_mate = swapped(pay_mate, 1)
    return call(
        decode_kernel,
        [VM] * 12,
        [shape((C1, ZD, YD, XD))],
        [
            V((32, NL), F32),
            V((2304, 8 * XC), BF),
            V((2, C1 * YD, XC), F32),
            V((CHIP, TILE), F32),
            V((ZD, C1, YD, XD), BF),
            pltpu.SemaphoreType.DMA((ZD,)),
        ],
        outs_in=ANY,
        cost=cost(5.0),
        vlim=24 * MIB,
        name="decode",
    )(win, got_near, got_far, got_mate, beyond, fs, fh, flat, wdec, wb, mats, small)[0]


def solution(mesh):
    in_specs = (
        P(None, "gz", "gy", None),
        P("gz", None, None),
        P(),
        P("gy", None, None),
        P("gy", None, None),
        P("gy", None, None),
        P("gy", None, None),
        P(),
        P(),
    )
    out_specs = P(None, "gz", "gy", None)
    return jax.shard_map(
        per_device, mesh=mesh, in_specs=in_specs, out_specs=out_specs, check_vma=False
    )
```

```python
import functools

import jax
import jax.numpy as jnp
from jax import lax
from jax.experimental import pallas as pl
from jax.experimental.pallas import tpu as pltpu
from jax.sharding import PartitionSpec as P

C1, C2 = 32, 64
ZD, YD, XD = 4, 16, 256
XC = XD // 2
SPAN = 7
NPD = 224
VIEWS = 4
NB = 64
DC = 768
TILE = 512
KL = 256
ROWS = 10
NL = ROWS * XC
CHIP = 12 * ROWS
OWN = 8 * ROWS
FAR = 6 * ROWS
MATE = 10 * ROWS
LIST = 256
BF, F32, I32 = jnp.bfloat16, jnp.float32, jnp.int32
MIB = 1024 * 1024


def dot(a, b):
    return jnp.dot(a, b, preferred_element_type=F32)


def iota(shape, dim):
    return lax.broadcasted_iota(I32, shape, dim)


def split_columns():
    row, col = iota((XD, XD), 0), iota((XD, XD), 1)
    return (row == 2 * (col % XC) + col // XC).astype(BF)


def merge_columns():
    row, col = iota((XD, XD), 0), iota((XD, XD), 1)
    return (col == 2 * (row % XC) + row // XC).astype(BF)


def edge_kernel(counts, block, tile, view, state, up, down, own, lists, cs, pairs, planes, sems):
    slab = lax.axis_index("gz")
    at = pl.multiple_of((slab // 8) * 8, 8)
    copies = [pltpu.make_async_copy(counts, cs, sems.at[0])]
    for i, ref in enumerate((block, tile, view)):
        copies.append(pltpu.make_async_copy(ref.at[0, pl.ds(at, 8)], pairs.at[i], sems.at[1 + i]))
    for z in range(ZD):
        copies.append(pltpu.make_async_copy(state.at[:, z], planes.at[z], sems.at[4 + z]))
    for copy in copies:
        copy.start()
    row, col = iota((4 * C1, C1 * YD), 0), iota((4 * C1, C1 * YD), 1)
    y = row // C1
    y = jnp.where(y < 2, y, y + YD - 4)
    pick = (col == (row % C1) * YD + y).astype(BF)
    lists[...] = jnp.full((16, KL), -1.0, F32)
    own[...] = jnp.full((8, KL), -1, I32)
    for copy in copies[:4]:
        copy.wait()
    slot = iota((1, NPD), 1)
    group = jnp.zeros((1, NPD), I32)
    end = 0
    for o in range(SPAN):
        end = end + cs[o, 0, slab]
        group = group + (slot >= end).astype(I32)
    valid = group < SPAN
    rest = pl.ds(slab % 8, 1)
    b, t, v = pairs[0, rest, :], pairs[1, rest, :], pairs[2, rest, :]
    key = v * NB + b
    own[0:1, :NPD] = key
    own[1:2, :NPD] = jnp.where(valid, group * 16 + t + 1, -1)
    lists[0:1, :NPD] = key.astype(F32)
    lists[1:2, :NPD] = jnp.where(valid & (t == 7), group, -1).astype(F32)
    up[LIST:, :] = lists[...].astype(BF)
    lists[1:2, :NPD] = jnp.where(valid & (t == 0), group, -1).astype(F32)
    down[LIST:, :] = lists[...].astype(BF)
    for z in range(ZD):
        copies[4 + z].wait()
        rows = dot(pick, planes[z].reshape(C1 * YD, XD)).astype(BF)
        down[z * 64 : z * 64 + 64, :] = rows[:64]
        up[z * 64 : z * 64 + 64, :] = rows[64:]


def project_kernel(res, proj, flat, high, low):
    y = dot(res[...].reshape(4 * NB, DC), proj[0])
    hi = y.astype(BF)
    lo = (y - hi.astype(F32)).astype(BF)
    for r in range(4):
        high[r] = hi[r * NB : (r + 1) * NB]
        low[r] = lo[r * NB : (r + 1) * NB]


def flat_kernel(state, flat):
    split = split_columns()
    for z in range(ZD):
        flat[z] = dot(state[:, z].reshape(C1 * YD, XD), split).astype(BF)


def place_kernel(own, left, right, high, low, fs, win, near, far, mate, out, keys):
    slab, part = lax.axis_index("gz"), lax.axis_index("gy")
    core = slab % 2
    keys[0:1, 0:KL] = own[0:1, :].astype(F32)
    keys[1:2, 0:KL] = own[1:2, :].astype(F32)
    lk = left[LIST:, :].astype(F32)
    rk = right[LIST:, :].astype(F32)
    keys[0:1, KL : 2 * KL] = lk[0:1]
    keys[0:1, 2 * KL :] = rk[0:1]
    lg, rg = lk[1:2], rk[1:2]
    keys[1:2, KL : 2 * KL] = jnp.where((lg >= 0) & (part > 0), lg * 16, -1.0)
    keys[1:2, 2 * KL :] = jnp.where((rg >= 0) & (part < 3), rg * 16 + 9, -1.0)
    key = keys[0:1, :].astype(I32)
    skey = keys[1:2, :].astype(I32)
    total = 416
    row = iota((total, 1), 0)

    def pieces(values):
        w, n, m, f = values
        return jnp.where(row < 120, w, jnp.where(row < 240, n, jnp.where(row < 352, m, f)))

    k = row - pieces((0, 120, 240, 352))
    t = k // ROWS
    n = k % ROWS
    even = core == 0
    first = jnp.where(even, pieces((-2, 1, 6, -7)), pieces((5, 2, -3, 10)))
    step = jnp.where(even, pieces((1, -1, 1, -1)), pieces((-1, 1, -1, 1)))
    s = first + step * t + 12
    rkey = jnp.where(t < pieces((12, 12, 10, 6)), (s // 4) * 16 + n, -2)
    r = s % 4
    a = (rkey == skey).astype(BF)
    bk = (iota((VIEWS * NB, 1), 0) == key).astype(BF)
    count = lax.dot_general(a, bk, (((1,), (1,)), ((), ())), preferred_element_type=F32)
    each = jnp.concatenate([jnp.where(r == q, count, 0.0).astype(BF) for q in range(4)], axis=1)
    acc = dot(each, high[...].reshape(4 * VIEWS * NB, TILE)) + dot(each, low[...].reshape(4 * VIEWS * NB, TILE))
    win[...] = acc[:120]
    near[...] = acc[120:240]
    mate[...] = acc[240:352].astype(BF)
    far[...] = acc[352:]
    for t in range(4):
        out[t * C2 : (t + 1) * C2, :] = fs[core, :, t * XD : (t + 1) * XD].astype(BF)


def encode_kernel(flat, enc, fs, wb, we, x, wide):
    rows = iota((32, C2), 0)
    bias = [jnp.zeros((32, C2), F32) for _ in range(4)]
    for p in range(2):
        for q in range(2):
            e = enc[p, q].astype(F32)
            for s in range(2):
                k = p * 4 + q * 2 + s
                es = e[:, s, :]
                we[k * C1 : (k + 1) * C1, :] = es[:C1].astype(BF)
                for a in range(4):
                    bias[a] = bias[a] + jnp.where(rows == (q * 2 + s) * 8 + 2 * a + p, es[C1 : C1 + 1], 0.0)
    for a in range(4):
        wb[a] = bias[a].astype(BF)
    for z in range(ZD):
        for s in range(2):
            wide[z * 2 + s] = flat[z, :, s * XC : (s + 1) * XC].astype(F32)
    for a in range(2):
        for p in range(2):
            z = 2 * a + p
            for q in range(2):
                for s in range(2):
                    k = (p * 4 + q * 2 + s) * C1
                    for b in range(8):
                        y = wide[z * 2 + s, pl.ds(2 * b + q, C1, stride=YD), :]
                        x[k : k + C1, b * XC : (b + 1) * XC] = y.astype(BF)
        f = lax.dot_general(we[...], x[...], (((0,), (0,)), ((), ())), preferred_element_type=F32)
        fs[a] = f


def halo_kernel(left, right, we, fs, fh, edge, keep, x):
    split = split_columns()
    before = dot(left[:LIST, :], split).astype(BF)
    after = dot(right[:LIST, :], split).astype(BF)
    for a in range(2):
        for p in range(2):
            for q in range(2):
                for s in range(2):
                    k = (p * 4 + q * 2 + s) * C1
                    lanes = slice(s * XC, (s + 1) * XC)
                    h = (2 * a + p) * 64 + q * C1
                    x[k : k + C1, 2 * a * XC : (2 * a + 1) * XC] = before[h : h + C1, lanes]
                    x[k : k + C1, (2 * a + 1) * XC : (2 * a + 2) * XC] = after[h : h + C1, lanes]
    f = lax.dot_general(we[...], x[...], (((0,), (0,)), ((), ())), preferred_element_type=F32)
    for a in range(2):
        fh[a] = f[:, a * XD : (a + 1) * XD]
    core = lax.axis_index("gz") % 2
    edge[...] = fh[core].astype(BF)
    for t in range(4):
        keep[t * C2 : (t + 1) * C2, :] = fs[1 - core, :, t * XD : (t + 1) * XD].astype(BF)
    keep[4 * C2 :, :] = fh[1 - core].astype(BF)


def prepare_kernel(dec, beyond, wdec, mats, small):
    mats[0:XD, 0:XD] = split_columns()
    mats[0:XD, XD : 2 * XD] = merge_columns()
    core = lax.axis_index("gz") % 2
    row, col = iota((OWN, OWN), 0), iota((OWN, OWN), 1)
    small[0] = ((col % ROWS == row % ROWS) & (col // ROWS == 7 - row // ROWS)).astype(BF)
    z = row % 8
    z = jnp.where(core == 0, z, 7 - z)
    small[1] = ((col % ROWS == row // 8) & (col // ROWS == z)).astype(BF)
    wdec[...] = jnp.zeros_like(wdec)
    taps = (((0, 3), (1, 1)), ((1, 2), (2, 0)))
    for pz in range(2):
        for sel in range(2):
            kz = taps[pz][sel][1]
            for py in range(2):
                for dy, ky in taps[py]:
                    for px in range(2):
                        for dx, kx in taps[px]:
                            r0 = (py * 2 + px) * C1
                            c0 = (sel * 9 + dy * 3 + dx) * C2
                            wdec[pz, r0 : r0 + C1, c0 : c0 + C2] = dec[kz, ky, kx]


def out_kernel(near, far, got, edge, pay, pay_far, tmp):
    tmp[0:CHIP] = near[...]
    tmp[CHIP:128] = jnp.zeros((8, TILE), F32)
    tmp[0:MATE] += got[...].astype(F32)[:MATE]
    total = tmp[...].astype(BF)
    pay[0:128, :] = total[:, :XD]
    pay[128:256, :] = total[:, XD:]
    pay[256:, :] = edge[...]
    tmp[0:64] = far[...]
    tmp[0 : 2 * ROWS] += got[...].astype(F32)[8 * ROWS : MATE]
    pay_far[...] = tmp[0:64].astype(BF)


def add_near(tmp, win, near):
    tmp[:, :XD] = win[:, :XD] + near[0:128, :].astype(F32)[:CHIP]
    tmp[:, XD:] = win[:, XD:] + near[128:256, :].astype(F32)[:CHIP]


def mate_kernel(win, near, far, pre, small, pay, tmp):
    add_near(tmp, win, near)
    tmp[0:64] += far[...].astype(F32)
    total = tmp[CHIP - OWN :, :].astype(BF)
    pay[0:OWN, :] = total[:, :XD]
    pay[OWN : 2 * OWN, :] = total[:, XD:]
    pay[2 * OWN :, :] = pre[...]


def decode_kernel(win, near, far, mate, beyond, fs, fh, flat, wdec, wb, mats, small, out, bp, x, ns, tmp, stage, sems):
    slab, part = lax.axis_index("gz"), lax.axis_index("gy")
    core = slab % 2
    split = mats[0:XD, 0:XD]
    merge = mats[0:XD, XD : 2 * XD]
    turn, sort = small[0], small[1]
    add_near(tmp, win, near)
    tmp[0:64] += far[...].astype(F32)
    for q in range(2):
        t = tmp[0:OWN, q * XD : (q + 1) * XD] + dot(turn, mate[q * OWN : (q + 1) * OWN, :])
        t = dot(dot(sort, t.astype(BF)).astype(BF), split)
        for s in range(2):
            for n in range(ROWS):
                bp[(q * 2 + s) * 8 : (q * 2 + s + 1) * 8, n * XC : (n + 1) * XC] = t[
                    n * 8 : (n + 1) * 8, s * XC : (s + 1) * XC
                ]
    bpb = bp[...].astype(BF)
    lane = iota((C2, XC), 1)
    for a in range(4):
        pb = lax.dot_general(wb[a], bpb, (((0,), (0,)), ((), ())), preferred_element_type=F32)
        inside = True
        if a == 0:
            inside = slab > 0
        if a == 3:
            inside = slab < 63
        for n in range(ROWS):
            outer = n in (0, 9)
            half = slice((n != 0) * XC, ((n != 0) + 1) * XC) if outer else slice((n - 1) % 2 * XC, ((n - 1) % 2 + 1) * XC)
            if a in (1, 2):
                v = fh[a - 1, :, half] if outer else fs[a - 1, :, (n - 1) * XC : n * XC]
            else:
                r0 = 4 * C2 if outer else (n - 1) // 2 * C2
                v1 = (near[256:, half] if outer else beyond[r0 : r0 + C2, half]).astype(F32)
                v2 = mate[2 * OWN + r0 : 2 * OWN + r0 + C2, half].astype(F32)
                v = jnp.where(core == (0 if a == 0 else 1), v1, v2)
            v = v + pb[:, n * XC : (n + 1) * XC]
            v = 0.5 * v * (1.0 + jnp.tanh(0.79788456 * (v + 0.044715 * (v * v * v))))
            ok = inside
            if n == 0:
                ok = (part > 0) & ok
            if n == 9:
                ok = (part < 3) & ok
            if ok is not True:
                v = jnp.where(ok, v, 0.0)
            shifts = (
                jnp.where(lane == 0, 0.0, pltpu.roll(v, 1, 1)).astype(BF),
                v.astype(BF),
                jnp.where(lane == XC - 1, 0.0, pltpu.roll(v, XC - 1, 1)).astype(BF),
            )
            for dy in range(3):
                m = n - dy
                if 0 <= m < 8:
                    for dx in range(3):
                        r0 = a * 576 + dy * 192 + dx * C2
                        x[r0 : r0 + C2, m * XC : (m + 1) * XC] = shifts[dx]
    middle = dot(wdec[...].reshape(256, 1152), x[576:1728, :])
    for f in range(ZD):
        if f in (1, 2):
            d = middle[128:] if f == 1 else middle[:128]
        else:
            d = dot(wdec[f % 2], x[f // 2 * 1152 : f // 2 * 1152 + 1152, :])
        for py in range(2):
            for px in range(2):
                r0 = (py * 2 + px) * C1
                for m in range(8):
                    ns[px, pl.ds(2 * m + py, C1, stride=YD), :] = d[r0 : r0 + C1, m * XC : (m + 1) * XC]
        both = jnp.concatenate([ns[0], ns[1]], axis=1)
        new = dot((flat[f].astype(F32) + both).astype(BF), merge).astype(BF)
        stage[f] = new.reshape(C1, YD, XD)
        pltpu.make_async_copy(stage.at[f], out.at[:, f], sems.at[f]).start()
    for f in range(ZD):
        pltpu.make_async_copy(stage.at[f], out.at[:, f], sems.at[f]).wait()


V = pltpu.VMEM
VM = pl.BlockSpec(memory_space=pltpu.VMEM)
ANY = pl.BlockSpec(memory_space=pl.ANY)


def shape(dims, dtype=BF):
    return jax.ShapeDtypeStruct(dims, dtype)


def call(kernel, ins, outs, scratch=(), cost=None, vlim=16 * MIB, outs_in=VM, **more):
    return pl.pallas_call(
        kernel,
        in_specs=ins,
        out_specs=[outs_in] * len(outs) if "grid" not in more else more.pop("specs"),
        out_shape=outs,
        scratch_shapes=scratch,
        compiler_params=pltpu.CompilerParams(vmem_limit_bytes=vlim),
        cost_estimate=cost,
        **more,
    )


def cost(us):
    return pl.CostEstimate(flops=int(us * 1e9), bytes_accessed=int(us * 3e6), transcendentals=0)


def shifted(block, axis, distance):
    n = lax.axis_size(axis)
    return lax.ppermute(block, axis, [(i, (i + distance) % n) for i in range(n)])


def swapped(block, distance):
    n, m = lax.axis_size("gz"), lax.axis_size("gy")
    pairs = {(i, i + distance) for i in range(0, n, 2) if 0 <= i + distance < n}
    if distance == -3:
        pairs |= {(0, 2), (n - 3, n - 1)}
    pairs = {(i * m + k, j * m + k) for i, j in pairs for k in range(m)}
    if distance == -1:
        pairs |= {(i * m + k, i * m + k + 1) for i in (0, n - 1) for k in range(0, m, 2)}
    return lax.ppermute(block, ("gz", "gy"), sorted(pairs | {(j, i) for i, j in pairs}))


def per_device(
    state, residual, projector, pair_counts, pair_block, pair_tile, pair_view, enc_weight, dec_weight
):
    up, down, own = call(
        edge_kernel,
        [ANY] * 5,
        [shape((272, XD)), shape((272, XD)), shape((8, KL), I32)],
        [
            V((16, KL), F32),
            pltpu.SMEM((SPAN, 1, 64), I32),
            V((3, 8, NPD), I32),
            V((ZD, C1, YD, XD), BF),
            pltpu.SemaphoreType.DMA((8,)),
        ],
        cost=cost(2.9),
        vlim=56 * MIB,
        name="edge",
    )(jnp.transpose(pair_counts, (2, 0, 1)), pair_block, pair_tile, pair_view, state)
    left = shifted(up, "gy", 1)
    right = shifted(down, "gy", -1)
    flat = call(flat_kernel, [VM], [shape((ZD, C1 * YD, XD))], cost=cost(0.4), name="flat")(state)[0]
    rays = jnp.transpose(residual, (1, 0, 2))
    high, low = call(
        project_kernel,
        [
            pl.BlockSpec((4, NB, DC), lambda v: (0, 0, 0)),
            pl.BlockSpec((1, DC, TILE), lambda v: (v, 0, 0)),
            ANY,
        ],
        [shape((4, VIEWS * NB, TILE)), shape((4, VIEWS * NB, TILE))],
        cost=cost(1.7),
        grid=(VIEWS,),
        specs=[pl.BlockSpec((4, NB, TILE), lambda v: (0, v, 0))] * 2,
        name="project",
    )(rays, projector, flat)
    fs, wb, we = call(
        encode_kernel,
        [VM] * 2,
        [shape((2, C2, 8 * XC), F32), shape((4, 32, C2)), shape((8 * C1, C2))],
        [V((8 * C1, 8 * XC), BF), V((2 * ZD, C1 * YD, XC), F32)],
        cost=cost(1.3),
        name="encode",
    )(flat, jnp.transpose(enc_weight, (0, 1, 4, 2, 3)))
    win, near, far, mate, pre_out = call(
        place_kernel,
        [VM] * 6,
        [
            shape((CHIP, TILE), F32),
            shape((CHIP, TILE), F32),
            shape((64, TILE), F32),
            shape((112, TILE)),
            shape((4 * C2, XD)),
        ],
        [V((8, 3 * KL), F32)],
        cost=cost(1.5),
        name="place",
    )(own, left, right, high, low, fs)
    got = swapped(mate, 1)
    beyond = swapped(pre_out, -1)
    fh, edge, pre_mate = call(
        halo_kernel,
        [VM] * 4,
        [shape((2, C2, XD), F32), shape((C2, XD)), shape((5 * C2, XD))],
        [V((8 * C1, 4 * XC), BF)],
        cost=cost(0.5),
        name="halo",
    )(left, right, we, fs)
    pay, pay_far = call(
        out_kernel,
        [VM] * 4,
        [shape((320, XD)), shape((64, TILE))],
        [V((128, TILE), F32)],
        cost=cost(0.1),
        name="outward",
    )(near, far, got, edge)
    got_near = swapped(pay, -1)
    got_far = swapped(pay_far, -3)
    wdec, mats, small = call(
        prepare_kernel,
        [VM, ANY],
        [shape((2, 128, 1152)), shape((XD, 2 * XD)), shape((2, OWN, OWN))],
        cost=cost(4.0),
        name="prepare",
    )(dec_weight, beyond)
    pay_mate = call(
        mate_kernel,
        [VM] * 4 + [ANY],
        [shape((2 * OWN + 5 * C2, XD))],
        [V((CHIP, TILE), F32)],
        cost=cost(0.1),
        name="inward",
    )(win, got_near, got_far, pre_mate, small)[0]
    got_mate = swapped(pay_mate, 1)
    return call(
        decode_kernel,
        [VM] * 12,
        [shape((C1, ZD, YD, XD))],
        [
            V((32, NL), F32),
            V((2304, 8 * XC), BF),
            V((2, C1 * YD, XC), F32),
            V((CHIP, TILE), F32),
            V((ZD, C1, YD, XD), BF),
            pltpu.SemaphoreType.DMA((ZD,)),
        ],
        outs_in=ANY,
        cost=cost(5.0),
        vlim=24 * MIB,
        name="decode",
    )(win, got_near, got_far, got_mate, beyond, fs, fh, flat, wdec, wb, mats, small)[0]


def solution(mesh):
    in_specs = (
        P(None, "gz", "gy", None),
        P("gz", None, None),
        P(),
        P("gy", None, None),
        P("gy", None, None),
        P("gy", None, None),
        P("gy", None, None),
        P(),
        P(),
    )
    out_specs = P(None, "gz", "gy", None)
    return jax.shard_map(
        per_device, mesh=mesh, in_specs=in_specs, out_specs=out_specs, check_vma=False
    )
```
